256 devices in a mesh: row: 16 (over z, y_lo), col: 16 (over x, y_hi, core).
Axes of the slice: x: 4, y: 4 (y_hi: 2, y_lo: 2; y = y_hi * 2 + y_lo), z: 8, core: 2. Of those that a mesh axis runs over, the one named last changes fastest.
Arguments:
- query_in: bfloat16 [2, 1536, 384], P(None, 'row'), may hold values from -10 to 10
- key_in: bfloat16 [2, 1536, 384], P(None, 'row'), may hold values from -10 to 10
- value_in: bfloat16 [2, 1536, 384], P(None, 'row'), may hold values from -6 to 6
- pair: bfloat16 [2, 1536, 1536, 128], P(None, 'row', 'col'), may hold values from -6 to 6
- bias_weight: bfloat16 [128, 16], replicated, may hold values from -0.5 to 0.5
- d_out: bfloat16 [2, 1536, 384], P(None, 'row'), may hold values from -192 to 192
Outputs:
- d_query: float32 [2, 1536, 384], P(None, 'row', 'col')
- d_key: float32 [2, 1536, 384], P(None, 'col', 'row')
- d_value: float32 [2, 1536, 384], P(None, 'col', 'row')
- d_pair: bfloat16 [2, 1536, 1536, 128], P(None, 'row', 'col')
- d_bias_weight: float32 [128, 16], replicated
The draws below stay inside these ranges and needn't reach their ends.
All inputs are finite; a program needn't handle non-finite values.
Results may differ from the reference program's by a relative error of at most 0.022.
Values may be sent and summed in bfloat16 or wider, within the bound.
No kernel may reach another device: no remote copies, remote signals or barrier semaphores. Data moves between devices by JAX's collectives and lax.ppermute only.
A program may use at most 64 MiB of HBM per device.

```python
import math
import jax
import jax.numpy as jnp
from jax import lax

H = 16
C = 24
CP = 128
B = 2
HC = 384
N = 1536


def aligned_rows(key):
    signs = jnp.where(jax.random.bernoulli(key, 0.5, (B, N, H * C)), 1.0, -1.0).astype(jnp.float32)
    positions = jnp.arange(N, dtype=jnp.int32)
    target = 160.0 + 25.0 * (positions // 16 % 3).astype(jnp.float32)
    level = jnp.sqrt(target / math.sqrt(C))
    picked = positions % 16 == 0
    return (signs, level, picked)


def base_field(key):
    return jnp.clip(jax.random.normal(key, (B, N, H * C), jnp.float32), -6.0, 6.0)


def draw_query_in(key, part):
    signs, level, picked = aligned_rows(key)
    key = jax.random.fold_in(key, 12)
    base = base_field(key)
    base = jnp.where(picked[None, :, None], level[None, :, None] * signs, base)
    return base.astype(jnp.bfloat16)


def draw_key_in(key, part):
    signs, level, picked = aligned_rows(key)
    key = jax.random.fold_in(key, 11)
    base = base_field(key)
    first = level[None, :, None] * signs
    prior_level = jnp.roll(level, 1)
    shrink = 1.0 - 2.0 / (prior_level * prior_level * math.sqrt(C))
    second = (prior_level * shrink)[None, :, None] * jnp.roll(signs, 1, axis=1)
    after = jnp.roll(picked, 1)
    base = jnp.where(picked[None, :, None], first, jnp.where(after[None, :, None], second, base))
    return base.astype(jnp.bfloat16)


def steps_of(rng, extent, split, low, high):
    def one(dim, blocks):
        steps = jax.random.uniform(jax.random.fold_in(jax.random.fold_in(rng, 6), dim), (blocks,), jnp.float32, low / len(split), high / len(split))
        return jnp.repeat(jnp.exp(steps), extent[dim] // blocks).reshape((-1,) + (1,) * (len(extent) - dim - 1))

    loudness = one(*split[0])
    for cut in split[1:]:
        loudness = loudness * one(*cut)
    return loudness


def gaussian(stream_key, dims, scale, most, pieces=(), held_as=jnp.bfloat16):
    values = scale * jax.random.normal(stream_key, dims, jnp.float32)
    if pieces:
        values = values * steps_of(stream_key, dims, pieces, -0.22, 0.18)
    return jnp.clip(values, -most, most).astype(held_as)


def setup_inputs(seed: int = 0) -> dict:
    key_list = jax.random.split(jax.random.key(seed), 7)
    query_in = draw_query_in(jax.random.fold_in(key_list[6], 71), 0)
    key_in = draw_key_in(jax.random.fold_in(key_list[6], 71), 0)
    value_in = gaussian(key_list[2], (B, N, HC), 1.0, 6.0, ((1, 16),))
    pair = gaussian(key_list[3], (B, N, N, CP), 1.0, 6.0, ((1, 16), (2, 16)))
    bias_weight = gaussian(key_list[4], (CP, H), CP ** -0.5, 0.5)
    d_out = gaussian(key_list[5], (B, N, HC), 32.0, 192.0, ((1, 16),))
    return dict(query_in=query_in, key_in=key_in, value_in=value_in, pair=pair, bias_weight=bias_weight, d_out=d_out)


EPS = 1e-05

def one_complex(query_one, key_one, value_one, pair_one, weight_float, grad_one):
    block = math.gcd(N, 128)
    score_scale = 1.0 / math.sqrt(C)
    key_heads = key_one.astype(jnp.float32).reshape(N, H, C)
    value_heads = value_one.astype(jnp.float32).reshape(N, H, C)
    starts = jnp.arange(N // block, dtype=jnp.int32) * block

    def step(carry, start):
        key_acc, value_acc, weight_acc = carry
        queries = lax.dynamic_slice_in_dim(query_one, start, block, 0).astype(jnp.float32).reshape(block, H, C)
        grads = lax.dynamic_slice_in_dim(grad_one, start, block, 0).astype(jnp.float32).reshape(block, H, C)
        pair_float = lax.dynamic_slice_in_dim(pair_one, start, block, 0).astype(jnp.float32)
        centre = lax.optimization_barrier(jnp.mean(pair_float, -1, keepdims=True))
        spread = lax.optimization_barrier(jnp.mean(jnp.square(pair_float - centre), -1, keepdims=True))
        inverse = lax.rsqrt(spread + EPS)
        normed = (pair_float - centre) * inverse
        normed_low = lax.optimization_barrier(normed.astype(jnp.bfloat16)).astype(jnp.float32)
        pair_bias = jnp.einsum('ijc,ch->hij', normed_low, weight_float)
        logits = jnp.einsum('ihc,jhc->hij', queries, key_heads) * score_scale + pair_bias
        row_top = lax.optimization_barrier(jnp.max(logits, -1, keepdims=True))
        expo = jnp.exp(logits - row_top)
        weights = expo / lax.optimization_barrier(jnp.sum(expo, -1, keepdims=True))
        d_weights = jnp.einsum('ihc,jhc->hij', grads, value_heads)
        balance = lax.optimization_barrier(jnp.sum(weights * d_weights, -1, keepdims=True))
        d_logits = weights * (d_weights - balance)
        ds_low = lax.optimization_barrier(d_logits.astype(jnp.bfloat16)).astype(jnp.float32)
        weights_low = lax.optimization_barrier(weights.astype(jnp.bfloat16)).astype(jnp.float32)
        query_grad = (jnp.einsum('hij,jhc->ihc', ds_low, key_heads) * score_scale).reshape(block, H * C)
        key_acc = key_acc + jnp.einsum('hij,ihc->jhc', ds_low, queries) * score_scale
        value_acc = value_acc + jnp.einsum('hij,ihc->jhc', weights_low, grads)
        weight_acc = weight_acc + jnp.einsum('ijc,hij->ch', normed_low, ds_low)
        pair_back = jnp.einsum('hij,ch->ijc', ds_low, weight_float)
        pair_grad = inverse * (pair_back - lax.optimization_barrier(jnp.mean(pair_back, -1, keepdims=True)) - normed * lax.optimization_barrier(jnp.mean(pair_back * normed, -1, keepdims=True)))
        return ((key_acc, value_acc, weight_acc), (query_grad, pair_grad.astype(jnp.bfloat16)))
    start_carry = (jnp.zeros((N, H, C), jnp.float32), jnp.zeros((N, H, C), jnp.float32), jnp.zeros((CP, H), jnp.float32))
    (key_acc, value_acc, weight_acc), (query_grads, pair_grads) = lax.scan(step, start_carry, starts)
    return (query_grads.reshape(N, H * C), key_acc.reshape(N, H * C), value_acc.reshape(N, H * C), pair_grads.reshape(N, N, CP), weight_acc)

def reference(query_in, key_in, value_in, pair, bias_weight, d_out):
    weight_float = bias_weight.astype(jnp.float32)
    results = [one_complex(query_in[member], key_in[member], value_in[member], pair[member], weight_float, d_out[member]) for member in range(B)]
    d_query = jnp.stack([item[0] for item in results])
    d_key = jnp.stack([item[1] for item in results])
    d_value = jnp.stack([item[2] for item in results])
    d_pair = jnp.stack([item[3] for item in results])
    d_bias_weight = results[0][4]
    for item in results[1:]:
        d_bias_weight = d_bias_weight + item[4]
    return (d_query, d_key, d_value, d_pair, d_bias_weight)
```

```python
import math

import jax
import jax.numpy as jnp
from jax import lax
from jax.experimental import pallas as pl
from jax.experimental.pallas import tpu as pltpu
from jax.sharding import PartitionSpec as P

EPS = 1e-05
F32 = jnp.float32
BF16 = jnp.bfloat16

B = 2
H = 16
C = 24
HC = H * C
CP = 128
T = 96
G = 12
I8 = 8
WIDE = I8 * CP
QH = T * H
SCALE = 1.0 / math.sqrt(C)
PEERS = 16

NN = (((1,), (0,)), ((), ()))
NT = (((1,), (1,)), ((), ()))
TN = (((0,), (0,)), ((), ()))


def dot(left, right, dims=NN):
    return lax.dot_general(left, right, dims, preferred_element_type=F32)


def iota(shape, dim):
    return lax.broadcasted_iota(jnp.int32, shape, dim)


def head_mask():
    row_head = (iota((HC, 128), 0) * 171) >> 12
    return row_head == (iota((HC, 128), 1) & (H - 1))


def query_lanes(rows, first):
    return jnp.where(iota((rows, QH), 0) - first == (iota((rows, QH), 1) >> 4), 1.0, 0.0).astype(BF16)


def block_diagonal(tile, rows_per_block):
    row_block = iota((128, CP), 0) // rows_per_block
    zero = jnp.zeros_like(tile)
    return jnp.concatenate([jnp.where(row_block == i, tile, zero) for i in range(I8)], axis=1)


def expand_kernel(q_ref, g_ref, qt_ref, gt_ref):
    lanes = query_lanes(T, 0)
    mask = head_mask()
    for source, target in ((q_ref, qt_ref), (g_ref, gt_ref)):
        for b in range(B):
            spread = dot(source[b], lanes, TN)
            for g in range(G):
                at = slice(g * 128, (g + 1) * 128)
                target[b, :, at] = jnp.where(mask, spread[:, at], 0.0).astype(BF16)


def norm_kernel(groups, pair_ref, wt_ref, n_ref, bias_ref, inv_ref, ones_ref, diag_ref):
    first = (pl.program_id(0) == 0) & (pl.program_id(1) == 0)

    @pl.when(first)
    def _():
        same = (iota((256, 256), 0) >> 7) == (iota((256, 256), 1) >> 7)
        ones_ref[...] = jnp.where(same, 1.0 / CP, 0.0).astype(BF16)
        wt = wt_ref[...].astype(F32)
        diag_ref[...] = block_diagonal(jnp.concatenate([wt] * I8, axis=0), H).astype(BF16)

    ones = ones_ref[...]
    lane_query = iota((T, 128), 1) >> 4
    for g in range(groups):
        halves = []
        compact = jnp.zeros((T, 128), F32)
        for p in range(I8 // 2):
            x = jnp.concatenate(
                [pair_ref[0, g * I8 + 2 * p], pair_ref[0, g * I8 + 2 * p + 1]], axis=1
            )
            centred = x.astype(F32) - dot(x, ones)
            spread = dot((centred * centred).astype(BF16), ones)
            inverse = lax.rsqrt(spread + EPS)
            normed = (centred * inverse).astype(BF16)
            n_ref[0, g, :, p * 256 : (p + 1) * 256] = normed
            halves.append(normed)
            for k in range(2):
                compact = jnp.where(
                    lane_query == 2 * p + k, inverse[:, k * CP : (k + 1) * CP], compact
                )
        inv_ref[0, g] = compact
        bias_ref[0, g] = dot(jnp.concatenate(halves, axis=1), diag_ref[...], NT)


def logits_kernel(k_ref, v_ref, qt_ref, gt_ref, bias_ref, logits_ref, dw_ref, stats_ref):
    for b in range(B):
        scores = dot(k_ref[b], qt_ref[b])
        inner = dot(v_ref[b], gt_ref[b])
        for g in range(G):
            at = slice(g * 128, (g + 1) * 128)
            logits = scores[:, at] * SCALE + bias_ref[b, g]
            dw = inner[:, at]
            logits_ref[b, g] = logits
            dw_ref[b, g] = dw
            top = jnp.max(logits, axis=0, keepdims=True)
            expo = jnp.exp(logits - top)
            total = jnp.sum(expo, axis=0, keepdims=True)
            level = top + jnp.log(total)
            balance = jnp.sum(expo * dw, axis=0, keepdims=True) / total
            row = b * 2 * G + g
            stats_ref[:, row : row + 1, :] = jnp.broadcast_to(level[None], (PEERS, 1, 128))
            stats_ref[:, row + G : row + G + 1, :] = jnp.broadcast_to(balance[None], (PEERS, 1, 128))


def grads_kernel(
    stats_ref, logits_ref, dw_ref, bias_ref, inv_ref, n_ref, qt_ref, gt_ref, k_ref,
    scaled_ref, along_ref, kv_ref, dq_ref, dwt_ref, ds_ref, w_ref,
):
    for b in range(B):
        levels = stats_ref[:, b * 2 * G : b * 2 * G + G, :]
        balances = stats_ref[:, b * 2 * G + G : (b + 1) * 2 * G, :]
        top = jnp.max(levels, axis=0)
        parts = jnp.exp(levels - top[None])
        total = jnp.sum(parts, axis=0)
        level = top + jnp.log(total)
        balance = jnp.sum(parts * balances, axis=0) / total
        for g in range(G):
            weights = jnp.exp(logits_ref[b, g] - level[g : g + 1])
            ds = weights * (dw_ref[b, g] - balance[g : g + 1])
            low = ds.astype(BF16)
            at = slice(g * 128, (g + 1) * 128)
            ds_ref[b, :, at] = low
            w_ref[b, :, at] = weights.astype(BF16)
            scaled = low.astype(F32) * inv_ref[b, g]
            scaled_ref[b, g] = scaled.astype(BF16)
            along_ref[b, g] = (scaled * bias_ref[b, g] * (1.0 / CP)).astype(BF16)

    total = jnp.zeros((128, WIDE), F32)
    for b in range(B):
        left = jnp.concatenate([ds_ref[b, :, g * 128 : (g + 1) * 128] for g in range(G)], axis=0)
        total = total + dot(left, n_ref[b].reshape(G * T, WIDE), TN)
    dwt = jnp.zeros((H, CP), F32)
    for i in range(I8):
        dwt = dwt + total[i * H : (i + 1) * H, i * CP : (i + 1) * CP]
    dwt_ref[...] = dwt

    mask = head_mask()
    keys, values = [], []
    queries = jnp.zeros((HC, 2 * T), F32)
    for b in range(B):
        keys.append(dot(qt_ref[b], ds_ref[b], NT) * SCALE)
        values.append(dot(gt_ref[b], w_ref[b], NT))
        spread = dot(k_ref[b], ds_ref[b], TN)
        chosen = jnp.concatenate(
            [
                jnp.where(mask, spread[:, g * 128 : (g + 1) * 128], 0.0).astype(BF16)
                for g in range(G)
            ],
            axis=1,
        )
        queries = queries + dot(chosen, query_lanes(2 * T, b * T), NT)
    kv = jnp.concatenate(keys + values, axis=1)
    queries = queries * SCALE
    high = dwt.astype(BF16)
    low = (dwt - high.astype(F32)).astype(BF16)
    for h in range(H):
        at = slice(h * C, (h + 1) * C)
        kv_ref[h, 0:C, :] = kv[at].astype(BF16)
        dq_ref[h] = queries[at].astype(BF16)
        kv_ref[h, C : C + H, :] = jnp.concatenate([high, low, jnp.zeros_like(low)], axis=1)


def pair_kernel(groups, scaled_ref, along_ref, n_ref, wt_ref, out_ref, ones_ref, diag_ref):
    first = (pl.program_id(0) == 0) & (pl.program_id(1) == 0)

    @pl.when(first)
    def _():
        ones_ref[...] = block_diagonal(jnp.ones((128, CP), F32), H).astype(BF16)
        wt = wt_ref[...].astype(F32)
        wt = wt - jnp.mean(wt, axis=1, keepdims=True)
        diag_ref[...] = block_diagonal(jnp.concatenate([wt] * I8, axis=0), H).astype(BF16)

    for g in range(groups):
        back = dot(scaled_ref[0, g], diag_ref[...])
        along = dot(along_ref[0, g], ones_ref[...])
        grad = (back - n_ref[0, g].astype(F32) * along).astype(BF16)
        for i in range(I8):
            out_ref[0, g * I8 + i] = grad[:, i * CP : (i + 1) * CP]


def keys_out_kernel(got_ref, dq_ref, key_ref, value_ref, send_ref):
    total = jnp.sum(got_ref[:, 0:C, :].astype(F32), axis=0)
    for b in range(B):
        key_ref[b] = total[:, b * T : (b + 1) * T]
        value_ref[b] = total[:, (B + b) * T : (B + b + 1) * T]
    parts = got_ref[:, C : C + H, 0 : 2 * CP].astype(F32)
    dwt = jnp.sum(parts[:, :, :CP] + parts[:, :, CP:], axis=0)
    high = dwt.astype(BF16)
    low = (dwt - high.astype(F32)).astype(BF16)
    both = jnp.concatenate([high, low], axis=1)
    for h in range(H):
        send_ref[h, 0:C, 0 : 2 * T] = dq_ref[h]
        send_ref[h, C : C + H, :] = both


def queries_out_kernel(got_ref, query_ref, dwt_ref):
    total = jnp.sum(got_ref[:, 0:C, 0 : 2 * T].astype(F32), axis=0)
    for b in range(B):
        query_ref[b] = total[:, b * T : (b + 1) * T]
    parts = got_ref[:, C : C + H, :].astype(F32)
    dwt_ref[...] = jnp.sum(parts[:, :, :CP] + parts[:, :, CP:], axis=0)


def call(kernel, outs, limit, flops=0, moved=0, **kw):
    return pl.pallas_call(
        kernel,
        out_shape=[jax.ShapeDtypeStruct(s, d) for s, d in outs],
        compiler_params=pltpu.CompilerParams(vmem_limit_bytes=limit << 20),
        cost_estimate=pl.CostEstimate(flops=flops, bytes_accessed=moved, transcendentals=0),
        **kw,
    )


def expand(query, grad):
    shape = ((B, HC, QH), BF16)
    return call(expand_kernel, [shape, shape], 24, flops=400_000_000, moved=5_000_000)(query, grad)


def norm(pair, wt):
    groups = 3
    spec = lambda *tail: pl.BlockSpec((1, groups, T) + tail, lambda b, s: (b, s, 0, 0))
    return call(
        lambda *refs: norm_kernel(groups, *refs),
        [((B, G, T, WIDE), BF16), ((B, G, T, 128), F32), ((B, G, T, 128), F32)],
        32,
        flops=4_000_000_000,
        moved=12_000_000,
        grid=(B, G // groups),
        in_specs=[
            pl.BlockSpec((1, groups * I8, T, CP), lambda b, s: (b, s, 0, 0)),
            pl.BlockSpec((H, CP), lambda b, s: (0, 0)),
        ],
        out_specs=[spec(WIDE), spec(128), spec(128)],
        scratch_shapes=[pltpu.VMEM((256, 256), BF16), pltpu.VMEM((128, WIDE), BF16)],
    )(pair, wt)


def logits(k, v, qt, gt, bias):
    big = ((B, G, T, 128), F32)
    return call(
        logits_kernel, [big, big, ((PEERS, 4 * G, 128), F32)], 32, flops=1_000_000_000, moved=8_000_000
    )(k, v, qt, gt, bias)


def grads(*args):
    return call(
        grads_kernel,
        [
            ((B, G, T, 128), BF16),
            ((B, G, T, 128), BF16),
            ((PEERS, C + H, 4 * T), BF16),
            ((PEERS, C, 2 * T), BF16),
            ((H, CP), F32),
        ],
        48,
        flops=4_000_000_000,
        moved=16_000_000,
        scratch_shapes=[pltpu.VMEM((B, T, QH), BF16), pltpu.VMEM((B, T, QH), BF16)],
    )(*args)


def pair_grad(scaled, along, n, wt):
    groups = 3
    spec = lambda *tail: pl.BlockSpec((1, groups, T) + tail, lambda b, s: (b, s, 0, 0))
    return call(
        lambda *refs: pair_kernel(groups, *refs),
        [((B, T, T, CP), BF16)],
        32,
        flops=4_000_000_000,
        moved=10_000_000,
        grid=(B, G // groups),
        in_specs=[spec(128), spec(128), spec(WIDE), pl.BlockSpec((H, CP), lambda b, s: (0, 0))],
        out_specs=[pl.BlockSpec((1, groups * I8, T, CP), lambda b, s: (b, s, 0, 0))],
        scratch_shapes=[pltpu.VMEM((128, WIDE), BF16), pltpu.VMEM((128, WIDE), BF16)],
    )(scaled, along, n, wt)[0]


def keys_out(got, dq):
    half = ((B, C, T), F32)
    return call(keys_out_kernel, [half, half, ((PEERS, C + H, 2 * CP), BF16)], 16)(got, dq)


def queries_out(got):
    return call(queries_out_kernel, [((B, C, T), F32), ((H, CP), F32)], 16)(got)


def key_route():
    pairs = []
    for row in range(PEERS):
        for col in range(PEERS):
            z, y_lo, core = row >> 1, row & 1, col & 1
            spot = (z - 2 * (col >> 1)) % 8
            pairs.append((col * PEERS + spot * 2 + y_lo, row * PEERS + col))
    return pairs


def spread_over(x, axis):
    return lax.all_to_all(x, axis, 0, 0, tiled=True)


def shards(query_in, key_in, value_in, pair, bias_weight, d_out):
    route = key_route()
    k = lax.ppermute(key_in, ("row", "col"), route)
    v = lax.ppermute(value_in, ("row", "col"), route)
    wt = bias_weight.T
    qt, gt = expand(query_in, d_out)
    n, bias, inv = norm(pair, wt)
    scores, dw, stats = logits(k, v, qt, gt, bias)
    stats = spread_over(stats, "col")
    scaled, along, kv, dq, _ = grads(stats, scores, dw, bias, inv, n, qt, gt, k)
    kv = spread_over(kv, "row")
    d_pair = pair_grad(scaled, along, n, wt)
    d_key, d_value, send = keys_out(kv, dq)
    d_query, dwt = queries_out(spread_over(send, "col"))
    flip = lambda x: jnp.swapaxes(x, 1, 2)
    return flip(d_query), flip(d_key), flip(d_value), d_pair, dwt.T


def solution(mesh):
    rows = P(None, "row", None)
    tiles = P(None, "row", "col", None)
    in_specs = (rows, rows, rows, tiles, P(), rows)
    swapped = P(None, "col", "row")
    out_specs = (P(None, "row", "col"), swapped, swapped, tiles, P())
    return jax.shard_map(shards, mesh=mesh, in_specs=in_specs, out_specs=out_specs, check_vma=False)
```

```python
import math

import jax
import jax.numpy as jnp
from jax import lax
from jax.experimental import pallas as pl
from jax.experimental.pallas import tpu as pltpu
from jax.sharding import PartitionSpec as P

EPS = 1e-05
F32 = jnp.float32
BF16 = jnp.bfloat16

B = 2
H = 16
C = 24
HC = H * C
CP = 128
T = 96
G = 12
I8 = 8
WIDE = I8 * CP
QH = T * H
SCALE = 1.0 / math.sqrt(C)
PEERS = 16
GROUPS = 6

NN = (((1,), (0,)), ((), ()))
NT = (((1,), (1,)), ((), ()))
TN = (((0,), (0,)), ((), ()))


def dot(left, right, dims=NN):
    return lax.dot_general(left, right, dims, preferred_element_type=F32)


def iota(shape, dim):
    return lax.broadcasted_iota(jnp.int32, shape, dim)


def head_mask():
    row_head = (iota((HC, 128), 0) * 171) >> 12
    return row_head == (iota((HC, 128), 1) & (H - 1))


def query_lanes(rows, first):
    return jnp.where(iota((rows, QH), 0) - first == (iota((rows, QH), 1) >> 4), 1.0, 0.0).astype(BF16)


def block_diagonal(tile, rows_per_block):
    row_block = iota((128, CP), 0) // rows_per_block
    zero = jnp.zeros_like(tile)
    return jnp.concatenate([jnp.where(row_block == i, tile, zero) for i in range(I8)], axis=1)


def expand(source, target):
    lanes = query_lanes(T, 0)
    mask = head_mask()
    for b in range(B):
        spread = dot(source[b], lanes, TN)
        for g in range(G):
            at = slice(g * 128, (g + 1) * 128)
            target[b, :, at] = jnp.where(mask, spread[:, at], 0.0).astype(BF16)


def expand_kernel(q_ref, g_ref, qt_ref, gt_ref):
    expand(q_ref, qt_ref)
    expand(g_ref, gt_ref)


def norm_kernel(groups, pair_ref, wt_ref, n_ref, bias_ref, inv_ref, ones_ref, diag_ref):
    first = (pl.program_id(0) == 0) & (pl.program_id(1) == 0)

    @pl.when(first)
    def _():
        same = (iota((256, 256), 0) >> 7) == (iota((256, 256), 1) >> 7)
        ones_ref[...] = jnp.where(same, 1.0 / CP, 0.0).astype(BF16)
        wt = wt_ref[...].astype(F32)
        diag_ref[...] = block_diagonal(jnp.concatenate([wt] * I8, axis=0), H).astype(BF16)

    ones = ones_ref[...]
    rows = groups * T
    lane_query = iota((rows, 128), 1) >> 4
    compact = jnp.zeros((rows, 128), F32)
    bias = jnp.zeros((rows, 128), F32)
    for p in range(I8 // 2):
        x = jnp.concatenate(
            [
                jnp.concatenate([pair_ref[0, g * I8 + 2 * p], pair_ref[0, g * I8 + 2 * p + 1]], axis=1)
                for g in range(groups)
            ],
            axis=0,
        )
        centred = x.astype(F32) - dot(x, ones)
        spread = dot((centred * centred).astype(BF16), ones)
        inverse = lax.rsqrt(spread + EPS)
        normed = (centred * inverse).astype(BF16)
        n_ref[0, :, :, p * 256 : (p + 1) * 256] = normed.reshape(groups, T, 256)
        for k in range(2):
            compact = jnp.where(
                lane_query == 2 * p + k, inverse[:, k * CP : (k + 1) * CP], compact
            )
        bias = bias + dot(normed, diag_ref[:, p * 256 : (p + 1) * 256], NT)
    inv_ref[0] = compact.reshape(groups, T, 128)
    bias_ref[0] = bias.reshape(groups, T, 128)


def logits_kernel(k_ref, v_ref, qt_ref, gt_ref, bias_ref, logits_ref, dw_ref, stats_ref):
    for b in range(B):
        scores = dot(k_ref[b], qt_ref[b])
        inner = dot(v_ref[b], gt_ref[b])
        for g in range(G):
            at = slice(g * 128, (g + 1) * 128)
            logits = scores[:, at] * SCALE + bias_ref[b, g]
            dw = inner[:, at]
            logits_ref[b, g] = logits
            dw_ref[b, g] = dw
            top = jnp.max(logits, axis=0, keepdims=True)
            expo = jnp.exp(logits - top)
            total = jnp.sum(expo, axis=0, keepdims=True)
            level = top + jnp.log(total)
            balance = jnp.sum(expo * dw, axis=0, keepdims=True) / total
            row = b * 2 * G + g
            stats_ref[:, row : row + 1, :] = jnp.broadcast_to(level[None], (PEERS, 1, 128))
            stats_ref[:, row + G : row + G + 1, :] = jnp.broadcast_to(balance[None], (PEERS, 1, 128))


def split_halves(x):
    high = x.astype(BF16)
    low = (x - high.astype(F32)).astype(BF16)
    return jnp.concatenate([high, low], axis=1)


def join_halves(parts):
    parts = parts.astype(F32)
    return jnp.sum(parts[:, :, :CP] + parts[:, :, CP:], axis=0)


def scores_kernel(
    stats_ref, logits_ref, dw_ref, bias_ref, inv_ref, k_ref, n_ref,
    ds_ref, w_ref, scaled_ref, along_ref, send_ref, n_here, n_sem,
):
    fetch = pltpu.make_async_copy(n_ref, n_here, n_sem)
    fetch.start()
    for b in range(B):
        levels = stats_ref[:, b * 2 * G : b * 2 * G + G, :]
        balances = stats_ref[:, b * 2 * G + G : (b + 1) * 2 * G, :]
        top = jnp.max(levels, axis=0)
        parts = jnp.exp(levels - top[None])
        total = jnp.sum(parts, axis=0)
        level = top + jnp.log(total)
        balance = jnp.sum(parts * balances, axis=0) / total
        for g in range(G):
            weights = jnp.exp(logits_ref[b, g] - level[g : g + 1])
            ds = weights * (dw_ref[b, g] - balance[g : g + 1])
            low = ds.astype(BF16)
            at = slice(g * 128, (g + 1) * 128)
            ds_ref[b, :, at] = low
            w_ref[b, :, at] = weights.astype(BF16)
            scaled = low.astype(F32) * inv_ref[b, g]
            scaled_ref[b, g] = scaled.astype(BF16)
            along_ref[b, g] = (scaled * bias_ref[b, g] * (1.0 / CP)).astype(BF16)

    mask = head_mask()
    queries = jnp.zeros((HC, 2 * T), F32)
    for b in range(B):
        spread = dot(k_ref[b], ds_ref[b], TN)
        chosen = jnp.concatenate(
            [
                jnp.where(mask, spread[:, g * 128 : (g + 1) * 128], 0.0).astype(BF16)
                for g in range(G)
            ],
            axis=1,
        )
        queries = queries + dot(chosen, query_lanes(2 * T, b * T), NT)
    queries = queries * SCALE

    fetch.wait()
    total = jnp.zeros((128, WIDE), F32)
    for b in range(B):
        left = jnp.concatenate([ds_ref[b, :, g * 128 : (g + 1) * 128] for g in range(G)], axis=0)
        total = total + dot(left, n_here[b].reshape(G * T, WIDE), TN)
    dwt = jnp.zeros((H, CP), F32)
    for i in range(I8):
        dwt = dwt + total[i * H : (i + 1) * H, i * CP : (i + 1) * CP]
    both = split_halves(dwt)
    for h in range(H):
        send_ref[h, 0:C, 0 : 2 * T] = queries[h * C : (h + 1) * C].astype(BF16)
        send_ref[h, C : C + H, :] = both


def grads_kernel(ds_ref, w_ref, q_ref, g_ref, kv_ref, qt_ref, gt_ref):
    expand(q_ref, qt_ref)
    expand(g_ref, gt_ref)
    keys = [dot(qt_ref[b], ds_ref[b], NT) * SCALE for b in range(B)]
    values = [dot(gt_ref[b], w_ref[b], NT) for b in range(B)]
    kv = jnp.concatenate(keys + values, axis=1)
    for h in range(H):
        kv_ref[h] = kv[h * C : (h + 1) * C].astype(BF16)


def pair_kernel(groups, scaled_ref, along_ref, n_ref, wt_ref, out_ref, ones_ref, diag_ref):
    first = (pl.program_id(0) == 0) & (pl.program_id(1) == 0)

    @pl.when(first)
    def _():
        ones_ref[...] = block_diagonal(jnp.ones((128, CP), F32), H).astype(BF16)
        wt = wt_ref[...].astype(F32)
        wt = wt - jnp.mean(wt, axis=1, keepdims=True)
        diag_ref[...] = block_diagonal(jnp.concatenate([wt] * I8, axis=0), H).astype(BF16)

    rows = groups * T
    scaled = scaled_ref[0].reshape(rows, 128)
    along = along_ref[0].reshape(rows, 128)
    for p in range(I8 // 2):
        at = slice(p * 256, (p + 1) * 256)
        back = dot(scaled, diag_ref[:, at])
        normed = n_ref[0, :, :, at].reshape(rows, 256).astype(F32)
        grad = (back - normed * dot(along, ones_ref[:, at])).astype(BF16)
        for g in range(groups):
            for k in range(2):
                out_ref[0, g * I8 + 2 * p + k] = grad[g * T : (g + 1) * T, k * CP : (k + 1) * CP]


def queries_out_kernel(got_ref, kv_ref, query_ref, send_ref):
    total = jnp.sum(got_ref[:, 0:C, 0 : 2 * T].astype(F32), axis=0)
    for b in range(B):
        query_ref[b] = total[:, b * T : (b + 1) * T]
    both = split_halves(join_halves(got_ref[:, C : C + H, :]))
    for h in range(H):
        send_ref[h, 0:C, :] = kv_ref[h]
        send_ref[h, C : C + H, 0 : 2 * CP] = both


def keys_out_kernel(got_ref, key_ref, value_ref, dwt_ref):
    total = jnp.sum(got_ref[:, 0:C, :].astype(F32), axis=0)
    for b in range(B):
        key_ref[b] = total[:, b * T : (b + 1) * T]
        value_ref[b] = total[:, (B + b) * T : (B + b + 1) * T]
    dwt_ref[...] = join_halves(got_ref[:, C : C + H, 0 : 2 * CP])


def call(kernel, outs, limit, flops=0, moved=0, **kw):
    return pl.pallas_call(
        kernel,
        out_shape=outs,
        compiler_params=pltpu.CompilerParams(vmem_limit_bytes=limit << 20),
        cost_estimate=pl.CostEstimate(flops=flops, bytes_accessed=moved, transcendentals=0),
        **kw,
    )


def f32(*shape):
    return jax.ShapeDtypeStruct(shape, F32)


def bf16(*shape):
    return jax.ShapeDtypeStruct(shape, BF16)


def far(*shape):
    return pltpu.HBM(shape, BF16)


def in_hbm(x):
    return pltpu.with_memory_space_constraint(x, pltpu.HBM)


def expanded(query, grad):
    shape = bf16(B, HC, QH)
    return call(expand_kernel, [shape, shape], 16, flops=400_000_000, moved=5_000_000)(query, grad)


def norm(pair, wt):
    groups = GROUPS
    spec = lambda *tail: pl.BlockSpec((1, groups, T) + tail, lambda b, s: (b, s, 0, 0))
    return call(
        lambda *refs: norm_kernel(groups, *refs),
        [far(B, G, T, WIDE), f32(B, G, T, 128), f32(B, G, T, 128)],
        24,
        flops=4_000_000_000,
        moved=12_000_000,
        grid=(B, G // groups),
        in_specs=[
            pl.BlockSpec((1, groups * I8, T, CP), lambda b, s: (b, s, 0, 0)),
            pl.BlockSpec((H, CP), lambda b, s: (0, 0)),
        ],
        out_specs=[spec(WIDE), spec(128), spec(128)],
        scratch_shapes=[pltpu.VMEM((256, 256), BF16), pltpu.VMEM((128, WIDE), BF16)],
    )(in_hbm(pair), wt)


def logits(k, v, qt, gt, bias):
    big = f32(B, G, T, 128)
    return call(
        logits_kernel, [big, big, f32(PEERS, 4 * G, 128)], 16, flops=1_000_000_000, moved=8_000_000
    )(k, v, qt, gt, bias)


def scores(*args):
    low = far(B, T, QH)
    cell = far(B, G, T, 128)
    whole = pl.BlockSpec(memory_space=pltpu.VMEM)
    return call(
        scores_kernel,
        [low, low, cell, cell, bf16(PEERS, C + H, 2 * CP)],
        24,
        flops=2_500_000_000,
        moved=8_000_000,
        in_specs=[whole] * 6 + [pl.BlockSpec(memory_space=pltpu.HBM)],
        out_specs=[whole] * 5,
        scratch_shapes=[pltpu.VMEM((B, G, T, WIDE), BF16), pltpu.SemaphoreType.DMA],
    )(*args)


def grads(*args):
    wide = pltpu.VMEM((B, HC, QH), BF16)
    return call(
        grads_kernel,
        [bf16(PEERS, C, 4 * T)],
        24,
        flops=2_500_000_000,
        moved=8_000_000,
        scratch_shapes=[wide, wide],
    )(*[in_hbm(x) for x in args])[0]


def pair_grad(scaled, along, n, wt):
    groups = GROUPS
    spec = lambda *tail: pl.BlockSpec((1, groups, T) + tail, lambda b, s: (b, s, 0, 0))
    return call(
        lambda *refs: pair_kernel(groups, *refs),
        [bf16(B, T, T, CP)],
        24,
        flops=4_000_000_000,
        moved=10_000_000,
        grid=(B, G // groups),
        in_specs=[spec(128), spec(128), spec(WIDE), pl.BlockSpec((H, CP), lambda b, s: (0, 0))],
        out_specs=[pl.BlockSpec((1, groups * I8, T, CP), lambda b, s: (b, s, 0, 0))],
        scratch_shapes=[pltpu.VMEM((128, WIDE), BF16), pltpu.VMEM((128, WIDE), BF16)],
    )(in_hbm(scaled), in_hbm(along), in_hbm(n), wt)[0]


def queries_out(got, kv):
    return call(queries_out_kernel, [f32(B, C, T), bf16(PEERS, C + H, 4 * T)], 16)(got, kv)


def keys_out(got):
    half = f32(B, C, T)
    return call(keys_out_kernel, [half, half, f32(H, CP)], 16)(got)


def ring_gap(size, a, b):
    return min((a - b) % size, (b - a) % size)


def hops(source, target):
    def place(index):
        row, col = divmod(index, PEERS)
        return row >> 1, col >> 2, (col >> 1 & 1) * 2 + (row & 1)

    (z, x, y), (z2, x2, y2) = place(source), place(target)
    return ring_gap(8, z, z2) + ring_gap(4, x, x2) + ring_gap(4, y, y2)


def key_route():
    pairs = []
    for col in range(PEERS):
        sources = [col * PEERS + k for k in range(PEERS)]
        targets = [row * PEERS + col for row in range(PEERS)]
        cost = [[hops(s, t) ** 3 for t in targets] for s in sources]
        chosen = list(range(PEERS))
        better = True
        while better:
            better = False
            for i in range(PEERS):
                for j in range(i):
                    now = cost[i][chosen[i]] + cost[j][chosen[j]]
                    then = cost[i][chosen[j]] + cost[j][chosen[i]]
                    if then < now:
                        chosen[i], chosen[j] = chosen[j], chosen[i]
                        better = True
        pairs += [(sources[i], targets[chosen[i]]) for i in range(PEERS)]
    return pairs


def spread_over(x, axis):
    return lax.all_to_all(x, axis, 0, 0, tiled=True)


def shards(query_in, key_in, value_in, pair, bias_weight, d_out):
    route = key_route()
    k = lax.ppermute(key_in, ("row", "col"), route)
    v = lax.ppermute(value_in, ("row", "col"), route)
    wt = bias_weight.T
    qt, gt = expanded(query_in, d_out)
    n, bias, inv = norm(pair, wt)
    scaled_scores, dw, stats = logits(k, v, qt, gt, bias)
    stats = spread_over(stats, "col")
    ds, w, scaled, along, send = scores(stats, scaled_scores, dw, bias, inv, k, n)
    got = spread_over(send, "col")
    kv = grads(ds, w, query_in, d_out)
    d_query, send = queries_out(got, kv)
    got = spread_over(send, "row")
    d_pair = pair_grad(scaled, along, n, wt)
    d_key, d_value, dwt = keys_out(got)
    flip = lambda x: jnp.swapaxes(x, 1, 2)
    return flip(d_query), flip(d_key), flip(d_value), d_pair, dwt.T


def solution(mesh):
    rows = P(None, "row", None)
    tiles = P(None, "row", "col", None)
    in_specs = (rows, rows, rows, tiles, P(), rows)
    swapped = P(None, "col", "row")
    out_specs = (P(None, "row", "col"), swapped, swapped, tiles, P())
    return jax.shard_map(shards, mesh=mesh, in_specs=in_specs, out_specs=out_specs, check_vma=False)
```

```python
import math

import jax
import jax.numpy as jnp
from jax import lax
from jax.experimental import pallas as pl
from jax.experimental.pallas import tpu as pltpu
from jax.sharding import PartitionSpec as P

EPS = 1e-05
F32 = jnp.float32
BF16 = jnp.bfloat16

B = 2
H = 16
C = 24
HC = H * C
CP = 128
T = 96
G = 12
I8 = 8
WIDE = I8 * CP
QH = T * H
SCALE = 1.0 / math.sqrt(C)
PEERS = 16
GROUPS = 6

NN = (((1,), (0,)), ((), ()))
NT = (((1,), (1,)), ((), ()))
TN = (((0,), (0,)), ((), ()))


def dot(left, right, dims=NN):
    return lax.dot_general(left, right, dims, preferred_element_type=F32)


def iota(shape, dim):
    return lax.broadcasted_iota(jnp.int32, shape, dim)


def head_mask():
    row_head = (iota((HC, 128), 0) * 171) >> 12
    return row_head == (iota((HC, 128), 1) & (H - 1))


def query_lanes(rows, first):
    return jnp.where(iota((rows, QH), 0) - first == (iota((rows, QH), 1) >> 4), 1.0, 0.0).astype(BF16)


def block_diagonal(tile, rows_per_block):
    row_block = iota((128, CP), 0) // rows_per_block
    zero = jnp.zeros_like(tile)
    return jnp.concatenate([jnp.where(row_block == i, tile, zero) for i in range(I8)], axis=1)


def expand(source, target):
    lanes = query_lanes(T, 0)
    mask = head_mask()
    for b in range(B):
        spread = dot(source[b], lanes, TN)
        for g in range(G):
            at = slice(g * 128, (g + 1) * 128)
            target[b, :, at] = jnp.where(mask, spread[:, at], 0.0).astype(BF16)


def expand_kernel(q_ref, g_ref, qt_ref, gt_ref, pick_ref):
    expand(q_ref, qt_ref)
    expand(g_ref, gt_ref)
    for b in range(B):
        pick_ref[:, b * QH : (b + 1) * QH] = query_lanes(B * T, b * T)


def norm_kernel(groups, pair_ref, wt_ref, n_ref, bias_ref, inv_ref, ones_ref, diag_ref):
    first = (pl.program_id(0) == 0) & (pl.program_id(1) == 0)

    @pl.when(first)
    def _():
        same = (iota((256, 256), 0) >> 7) == (iota((256, 256), 1) >> 7)
        ones_ref[...] = jnp.where(same, 1.0 / CP, 0.0).astype(BF16)
        wt = wt_ref[...].astype(F32)
        diag_ref[...] = block_diagonal(jnp.concatenate([wt] * I8, axis=0), H).astype(BF16)

    ones = ones_ref[...]
    rows = groups * T
    lane_query = iota((rows, 128), 1) >> 4
    compact = jnp.zeros((rows, 128), F32)
    bias = jnp.zeros((rows, 128), F32)
    for p in range(I8 // 2):
        x = jnp.concatenate(
            [
                jnp.concatenate([pair_ref[0, g * I8 + 2 * p], pair_ref[0, g * I8 + 2 * p + 1]], axis=1)
                for g in range(groups)
            ],
            axis=0,
        )
        centred = x.astype(F32) - dot(x, ones)
        spread = dot((centred * centred).astype(BF16), ones)
        inverse = lax.rsqrt(spread + EPS)
        normed = (centred * inverse).astype(BF16)
        n_ref[0, :, :, p * 256 : (p + 1) * 256] = normed.reshape(groups, T, 256)
        for k in range(2):
            compact = jnp.where(
                lane_query == 2 * p + k, inverse[:, k * CP : (k + 1) * CP], compact
            )
        bias = bias + dot(normed, diag_ref[:, p * 256 : (p + 1) * 256], NT)
    inv_ref[0] = compact.reshape(groups, T, 128)
    bias_ref[0] = bias.reshape(groups, T, 128)


def logits_kernel(k_ref, v_ref, qt_ref, gt_ref, bias_ref, logits_ref, dw_ref, stats_ref):
    for b in range(B):
        scores = dot(k_ref[b], qt_ref[b])
        inner = dot(v_ref[b], gt_ref[b])
        for g in range(G):
            at = slice(g * 128, (g + 1) * 128)
            logits = scores[:, at] * SCALE + bias_ref[b, g]
            dw = inner[:, at]
            logits_ref[b, g] = logits
            dw_ref[b, g] = dw
            top = jnp.max(logits, axis=0, keepdims=True)
            expo = jnp.exp(logits - top)
            total = jnp.sum(expo, axis=0, keepdims=True)
            level = top + jnp.log(total)
            balance = jnp.sum(expo * dw, axis=0, keepdims=True) / total
            row = b * 2 * G + g
            stats_ref[:, row : row + 1, :] = jnp.broadcast_to(level[None], (PEERS, 1, 128))
            stats_ref[:, row + G : row + G + 1, :] = jnp.broadcast_to(balance[None], (PEERS, 1, 128))


def split_halves(x):
    high = x.astype(BF16)
    low = (x - high.astype(F32)).astype(BF16)
    return jnp.concatenate([high, low], axis=1)


def join_halves(parts):
    parts = parts.astype(F32)
    return jnp.sum(parts[:, :, :CP] + parts[:, :, CP:], axis=0)


def scores_kernel(
    stats_ref, logits_ref, dw_ref, bias_ref, inv_ref, k_ref, pick_ref, n_ref,
    ds_ref, w_ref, scaled_ref, along_ref, send_ref, n_here, n_sem,
):
    fetch = pltpu.make_async_copy(n_ref, n_here, n_sem)
    fetch.start()
    for b in range(B):
        levels = stats_ref[:, b * 2 * G : b * 2 * G + G, :]
        balances = stats_ref[:, b * 2 * G + G : (b + 1) * 2 * G, :]
        top = jnp.max(levels, axis=0)
        parts = jnp.exp(levels - top[None])
        total = jnp.sum(parts, axis=0)
        level = top + jnp.log(total)
        balance = jnp.sum(parts * balances, axis=0) / total
        for g in range(G):
            weights = jnp.exp(logits_ref[b, g] - level[g : g + 1])
            ds = weights * (dw_ref[b, g] - balance[g : g + 1])
            low = ds.astype(BF16)
            at = slice(g * 128, (g + 1) * 128)
            ds_ref[b, :, at] = low
            w_ref[b, :, at] = weights.astype(BF16)
            scaled = low.astype(F32) * inv_ref[b, g]
            scaled_ref[b, g] = scaled.astype(BF16)
            along_ref[b, g] = (scaled * bias_ref[b, g] * (1.0 / CP)).astype(BF16)

    mask = head_mask()
    chosen = []
    for b in range(B):
        spread = dot(k_ref[b], ds_ref[b], TN)
        chosen += [
            jnp.where(mask, spread[:, g * 128 : (g + 1) * 128], 0.0).astype(BF16) for g in range(G)
        ]
    queries = dot(jnp.concatenate(chosen, axis=1), pick_ref[...], NT) * SCALE

    fetch.wait()
    total = jnp.zeros((128, WIDE), F32)
    for b in range(B):
        left = jnp.concatenate([ds_ref[b, :, g * 128 : (g + 1) * 128] for g in range(G)], axis=0)
        total = total + dot(left, n_here[b].reshape(G * T, WIDE), TN)
    dwt = jnp.zeros((H, CP), F32)
    for i in range(I8):
        dwt = dwt + total[i * H : (i + 1) * H, i * CP : (i + 1) * CP]
    both = split_halves(dwt)
    for h in range(H):
        send_ref[h, 0:C, 0 : 2 * T] = queries[h * C : (h + 1) * C].astype(BF16)
        send_ref[h, C : C + H, :] = both


def grads_kernel(ds_ref, w_ref, q_ref, g_ref, kv_ref, qt_ref, gt_ref):
    expand(q_ref, qt_ref)
    expand(g_ref, gt_ref)
    keys = [dot(qt_ref[b], ds_ref[b], NT) * SCALE for b in range(B)]
    values = [dot(gt_ref[b], w_ref[b], NT) for b in range(B)]
    kv = jnp.concatenate(keys + values, axis=1)
    for h in range(H):
        for t in range(3):
            part = kv[h * C : (h + 1) * C, t * 128 : (t + 1) * 128]
            kv_ref[h, t * C : (t + 1) * C, :] = part.astype(BF16)


def pair_kernel(groups, scaled_ref, along_ref, n_ref, wt_ref, out_ref, ones_ref, diag_ref):
    first = (pl.program_id(0) == 0) & (pl.program_id(1) == 0)

    @pl.when(first)
    def _():
        ones_ref[...] = block_diagonal(jnp.ones((128, CP), F32), H).astype(BF16)
        wt = wt_ref[...].astype(F32)
        wt = wt - jnp.mean(wt, axis=1, keepdims=True)
        diag_ref[...] = block_diagonal(jnp.concatenate([wt] * I8, axis=0), H).astype(BF16)

    rows = groups * T
    scaled = scaled_ref[0].reshape(rows, 128)
    along = along_ref[0].reshape(rows, 128)
    for p in range(I8 // 2):
        at = slice(p * 256, (p + 1) * 256)
        back = dot(scaled, diag_ref[:, at])
        normed = n_ref[0, :, :, at].reshape(rows, 256).astype(F32)
        grad = (back - normed * dot(along, ones_ref[:, at])).astype(BF16)
        for g in range(groups):
            for k in range(2):
                out_ref[0, g * I8 + 2 * p + k] = grad[g * T : (g + 1) * T, k * CP : (k + 1) * CP]


def queries_out_kernel(got_ref, kv_ref, query_ref, send_ref):
    total = jnp.sum(got_ref[:, 0:C, 0 : 2 * T].astype(F32), axis=0)
    for b in range(B):
        query_ref[b] = total[:, b * T : (b + 1) * T]
    dwt = join_halves(got_ref[:, C : C + H, :]).astype(BF16)
    send_ref[:, 0 : 3 * C, :] = kv_ref[...]
    for h in range(H):
        send_ref[h, 3 * C :, :] = dwt


def keys_out_kernel(got_ref, key_ref, value_ref, dwt_ref):
    total = jnp.sum(got_ref[...].astype(F32), axis=0)
    kv = jnp.concatenate([total[t * C : (t + 1) * C] for t in range(3)], axis=1)
    for b in range(B):
        key_ref[b] = kv[:, b * T : (b + 1) * T]
        value_ref[b] = kv[:, (B + b) * T : (B + b + 1) * T]
    dwt_ref[...] = total[3 * C :]


def call(kernel, outs, limit, flops=0, moved=0, **kw):
    return pl.pallas_call(
        kernel,
        out_shape=outs,
        compiler_params=pltpu.CompilerParams(vmem_limit_bytes=limit << 20),
        cost_estimate=pl.CostEstimate(flops=flops, bytes_accessed=moved, transcendentals=0),
        **kw,
    )


def f32(*shape):
    return jax.ShapeDtypeStruct(shape, F32)


def bf16(*shape):
    return jax.ShapeDtypeStruct(shape, BF16)


def far(*shape):
    return pltpu.HBM(shape, BF16)


def in_hbm(x):
    return pltpu.with_memory_space_constraint(x, pltpu.HBM)


def expanded(query, grad):
    shape = bf16(B, HC, QH)
    outs = [shape, shape, bf16(B * T, B * QH)]
    return call(expand_kernel, outs, 16, flops=400_000_000, moved=5_000_000)(query, grad)


def norm(pair, wt):
    groups = GROUPS
    spec = lambda *tail: pl.BlockSpec((1, groups, T) + tail, lambda b, s: (b, s, 0, 0))
    return call(
        lambda *refs: norm_kernel(groups, *refs),
        [far(B, G, T, WIDE), f32(B, G, T, 128), f32(B, G, T, 128)],
        24,
        flops=4_000_000_000,
        moved=12_000_000,
        grid=(B, G // groups),
        in_specs=[
            pl.BlockSpec((1, groups * I8, T, CP), lambda b, s: (b, s, 0, 0)),
            pl.BlockSpec((H, CP), lambda b, s: (0, 0)),
        ],
        out_specs=[spec(WIDE), spec(128), spec(128)],
        scratch_shapes=[pltpu.VMEM((256, 256), BF16), pltpu.VMEM((128, WIDE), BF16)],
    )(in_hbm(pair), in_hbm(wt))


def logits(k, v, qt, gt, bias):
    big = f32(B, G, T, 128)
    return call(
        logits_kernel, [big, big, f32(PEERS, 4 * G, 128)], 16, flops=1_000_000_000, moved=8_000_000
    )(k, v, qt, gt, bias)


def scores(*args):
    low = far(B, T, QH)
    cell = far(B, G, T, 128)
    whole = pl.BlockSpec(memory_space=pltpu.VMEM)
    return call(
        scores_kernel,
        [low, low, cell, cell, bf16(PEERS, C + H, 2 * CP)],
        24,
        flops=2_500_000_000,
        moved=8_000_000,
        in_specs=[whole] * 7 + [pl.BlockSpec(memory_space=pltpu.HBM)],
        out_specs=[whole] * 5,
        scratch_shapes=[pltpu.VMEM((B, G, T, WIDE), BF16), pltpu.SemaphoreType.DMA],
    )(*args)


def grads(*args):
    wide = pltpu.VMEM((B, HC, QH), BF16)
    return call(
        grads_kernel,
        [bf16(PEERS, 3 * C, 128)],
        24,
        flops=2_500_000_000,
        moved=8_000_000,
        scratch_shapes=[wide, wide],
    )(*[in_hbm(x) for x in args])[0]


def pair_grad(scaled, along, n, wt):
    groups = GROUPS
    spec = lambda *tail: pl.BlockSpec((1, groups, T) + tail, lambda b, s: (b, s, 0, 0))
    return call(
        lambda *refs: pair_kernel(groups, *refs),
        [bf16(B, T, T, CP)],
        24,
        flops=4_000_000_000,
        moved=10_000_000,
        grid=(B, G // groups),
        in_specs=[spec(128), spec(128), spec(WIDE), pl.BlockSpec((H, CP), lambda b, s: (0, 0))],
        out_specs=[pl.BlockSpec((1, groups * I8, T, CP), lambda b, s: (b, s, 0, 0))],
        scratch_shapes=[pltpu.VMEM((128, WIDE), BF16), pltpu.VMEM((128, WIDE), BF16)],
    )(in_hbm(scaled), in_hbm(along), in_hbm(n), in_hbm(wt))[0]


def queries_out(got, kv):
    return call(queries_out_kernel, [f32(B, C, T), bf16(PEERS, 3 * C + H, 128)], 16)(got, kv)


def keys_out(got):
    half = f32(B, C, T)
    return call(keys_out_kernel, [half, half, f32(H, CP)], 16)(got)


ROUTE = (
    "58b92a73e4d1c60f",
    "1986b504d32cf7ea",
    "db0a9542736e1f8c",
    "a8b163d74e5fc290",
    "0a71fcdbe6498253",
    "f32ecda57b861940",
    "352c1def8b6a9704",
    "745d0cfe28196a3b",
    "c695e478103f2adb",
    "d54a9762b1e0f38c",
    "f986a704c523d1eb",
    "eb7d48910263ac5f",
    "16fe0ad982bc5437",
    "73e01fc859ab462d",
    "f1253da0cb84e976",
    "c039e21bfad54876",
)


def key_route():
    return [
        (col * PEERS + k, int(digit, 16) * PEERS + col)
        for col, line in enumerate(ROUTE)
        for k, digit in enumerate(line)
    ]


def spread_over(x, axis):
    return lax.all_to_all(x, axis, 0, 0, tiled=True)


def shards(query_in, key_in, value_in, pair, bias_weight, d_out):
    route = key_route()
    k = lax.ppermute(key_in, ("row", "col"), route)
    v = lax.ppermute(value_in, ("row", "col"), route)
    wt = bias_weight.T
    qt, gt, pick = expanded(query_in, d_out)
    n, bias, inv = norm(pair, wt)
    scaled_scores, dw, stats = logits(k, v, qt, gt, bias)
    stats = spread_over(stats, "col")
    ds, w, scaled, along, send = scores(stats, scaled_scores, dw, bias, inv, k, pick, n)
    got = spread_over(send, "col")
    kv = grads(ds, w, query_in, d_out)
    d_query, send = queries_out(got, kv)
    got = spread_over(send, "row")
    d_pair = pair_grad(scaled, along, n, wt)
    d_key, d_value, dwt = keys_out(got)
    flip = lambda x: jnp.swapaxes(x, 1, 2)
    return flip(d_query), flip(d_key), flip(d_value), d_pair, dwt.T


def solution(mesh):
    rows = P(None, "row", None)
    tiles = P(None, "row", "col", None)
    in_specs = (rows, rows, rows, tiles, P(), rows)
    swapped = P(None, "col", "row")
    out_specs = (P(None, "row", "col"), swapped, swapped, tiles, P())
    return jax.shard_map(shards, mesh=mesh, in_specs=in_specs, out_specs=out_specs, check_vma=False)
```

```python
import math

import jax
import jax.numpy as jnp
from jax import lax
from jax.experimental import pallas as pl
from jax.experimental.pallas import tpu as pltpu
from jax.sharding import PartitionSpec as P

EPS = 1e-05
F32 = jnp.float32
BF16 = jnp.bfloat16

B = 2
H = 16
C = 24
HC = H * C
CP = 128
T = 96
G = 12
I8 = 8
WIDE = I8 * CP
QH = T * H
SCALE = 1.0 / math.sqrt(C)
PEERS = 16
PLANE = 2 * PEERS
DEPTH = 8
GROUPS = 6

NN = (((1,), (0,)), ((), ()))
NT = (((1,), (1,)), ((), ()))
TN = (((0,), (0,)), ((), ()))


def dot(left, right, dims=NN):
    return lax.dot_general(left, right, dims, preferred_element_type=F32)


def iota(shape, dim):
    return lax.broadcasted_iota(jnp.int32, shape, dim)


def head_mask():
    row_head = (iota((HC, 128), 0) * 171) >> 12
    return row_head == (iota((HC, 128), 1) & (H - 1))


def query_lanes(rows, first):
    return jnp.where(iota((rows, QH), 0) - first == (iota((rows, QH), 1) >> 4), 1.0, 0.0).astype(BF16)


def block_diagonal(tile, rows_per_block):
    row_block = iota((128, CP), 0) // rows_per_block
    zero = jnp.zeros_like(tile)
    return jnp.concatenate([jnp.where(row_block == i, tile, zero) for i in range(I8)], axis=1)


def expand(source, target):
    lanes = query_lanes(T, 0)
    mask = head_mask()
    for b in range(B):
        spread = dot(source[b], lanes, TN)
        for g in range(G):
            at = slice(g * 128, (g + 1) * 128)
            target[b, :, at] = jnp.where(mask, spread[:, at], 0.0).astype(BF16)


def expand_kernel(q_ref, g_ref, qt_ref, gt_ref, pick_ref, turn_ref):
    expand(q_ref, qt_ref)
    expand(g_ref, gt_ref)
    lane = iota((256, B * HC), 1)
    batch = jnp.where(lane >= HC, 1, 0)
    within = lane - batch * HC
    query = (within >> 7) * 32 + (within >> 2 & 3) * I8 + (within >> 4 & 7)
    pick_ref[...] = jnp.where(iota((256, B * HC), 0) == batch * T + query, 1.0, 0.0).astype(BF16)
    row = iota((2 * H * 16, HC), 0)
    feature = (row >> 5) * C + (row >> 4 & 1) * 12 + (row & 15)
    used = ((row & 15) < 12) & (iota((2 * H * 16, HC), 1) == feature)
    turn_ref[...] = jnp.where(used, 1.0, 0.0).astype(BF16)


def norm_kernel(groups, pair_ref, wt_ref, n_ref, bias_ref, inv_ref, ones_ref, diag_ref):
    first = (pl.program_id(0) == 0) & (pl.program_id(1) == 0)

    @pl.when(first)
    def _():
        same = (iota((256, 256), 0) >> 7) == (iota((256, 256), 1) >> 7)
        ones_ref[...] = jnp.where(same, 1.0 / CP, 0.0).astype(BF16)
        wt = wt_ref[...].astype(F32)
        diag_ref[...] = block_diagonal(jnp.concatenate([wt] * I8, axis=0), H).astype(BF16)

    ones = ones_ref[...]
    rows = groups * T
    lane_query = iota((rows, 128), 1) >> 4
    compact = jnp.zeros((rows, 128), F32)
    bias = jnp.zeros((rows, 128), F32)
    for p in range(I8 // 2):
        x = jnp.concatenate(
            [
                jnp.concatenate([pair_ref[0, g * I8 + 2 * p], pair_ref[0, g * I8 + 2 * p + 1]], axis=1)
                for g in range(groups)
            ],
            axis=0,
        )
        centred = x.astype(F32) - dot(x, ones)
        spread = dot((centred * centred).astype(BF16), ones)
        inverse = lax.rsqrt(spread + EPS)
        normed = (centred * inverse).astype(BF16)
        n_ref[0, :, :, p * 256 : (p + 1) * 256] = normed.reshape(groups, T, 256)
        for k in range(2):
            compact = jnp.where(
                lane_query == 2 * p + k, inverse[:, k * CP : (k + 1) * CP], compact
            )
        bias = bias + dot(normed, diag_ref[:, p * 256 : (p + 1) * 256], NT)
    inv_ref[0] = compact.reshape(groups, T, 128)
    bias_ref[0] = bias.reshape(groups, T, 128)


def logits_kernel(k_ref, v_ref, qt_ref, gt_ref, bias_ref, logits_ref, dw_ref, stats_ref):
    for b in range(B):
        scores = dot(k_ref[b], qt_ref[b])
        inner = dot(v_ref[b], gt_ref[b])
        for g in range(G):
            at = slice(g * 128, (g + 1) * 128)
            logits = scores[:, at] * SCALE + bias_ref[b, g]
            dw = inner[:, at]
            logits_ref[b, g] = logits
            dw_ref[b, g] = dw
            top = jnp.max(logits, axis=0, keepdims=True)
            expo = jnp.exp(logits - top)
            total = jnp.sum(expo, axis=0, keepdims=True)
            level = top + jnp.log(total)
            balance = jnp.sum(expo * dw, axis=0, keepdims=True) / total
            row = b * 2 * G + g
            stats_ref[:, row : row + 1, :] = jnp.broadcast_to(level[None], (PEERS, 1, 128))
            stats_ref[:, row + G : row + G + 1, :] = jnp.broadcast_to(balance[None], (PEERS, 1, 128))


def four_query(shape, dim):
    lane = iota(shape, dim)
    return (lane >> 7) * 32 + (lane >> 2 & 3) * I8 + (lane >> 4 & 7)


def four_heads(parts, q):
    slot = iota((T, 128), 1) >> 2 & 3
    tiles = []
    for wide in range(G // 4):
        tile = parts[wide * 4 + q]
        for k in range(4):
            if k != q:
                moved = pltpu.roll(parts[wide * 4 + k], (4 * (k - q)) % 128, 1)
                tile = jnp.where(slot == k, moved, tile)
        tiles.append(tile.astype(BF16))
    return jnp.concatenate(tiles, axis=1)


def scores_kernel(
    stats_ref, logits_ref, dw_ref, bias_ref, inv_ref, k_ref, pick_ref, turn_ref, n_ref,
    four_out, w_out, scaled_out, along_out, send_ref,
    ds_ref, four_ref, w_ref, scaled_ref, along_ref, sems,
):
    keep = iota((128, HC), 0) >> 5 == (iota((128, HC), 1) & 3)
    chosen = []
    for b in range(B):
        levels = stats_ref[:, b * 2 * G : b * 2 * G + G, :]
        balances = stats_ref[:, b * 2 * G + G : (b + 1) * 2 * G, :]
        top = jnp.max(levels, axis=0)
        parts = jnp.exp(levels - top[None])
        total = jnp.sum(parts, axis=0)
        level = top + jnp.log(total)
        balance = jnp.sum(parts * balances, axis=0) / total
        lows = []
        for g in range(G):
            weights = jnp.exp(logits_ref[b, g] - level[g : g + 1])
            ds = weights * (dw_ref[b, g] - balance[g : g + 1])
            low = ds.astype(BF16)
            at = slice(g * 128, (g + 1) * 128)
            ds_ref[b, :, at] = low
            w_ref[b, :, at] = weights.astype(BF16)
            low = low.astype(F32)
            lows.append(low)
            scaled = low * inv_ref[b, g]
            scaled_ref[b, g] = scaled.astype(BF16)
            along_ref[b, g] = (scaled * bias_ref[b, g] * (1.0 / CP)).astype(BF16)
        k_turned = dot(turn_ref[...], k_ref[b], NT).astype(BF16)
        quarters = []
        for q in range(4):
            four = four_heads(lows, q)
            four_ref[b, q] = four
            spread = dot(k_turned[q * 128 : (q + 1) * 128], four)
            quarters.append(jnp.where(keep, spread, 0.0).astype(BF16))
        chosen.append(jnp.concatenate(quarters, axis=0))
    pairs = ((four_ref, four_out), (w_ref, w_out), (scaled_ref, scaled_out), (along_ref, along_out))
    stores = [pltpu.make_async_copy(x, y, sems.at[i]) for i, (x, y) in enumerate(pairs)]
    for store in stores:
        store.start()
    queries = dot(jnp.concatenate(chosen, axis=1), pick_ref[...], NT) * SCALE

    total = jnp.zeros((128, WIDE), F32)
    for b in range(B):
        left = jnp.concatenate([ds_ref[b, :, g * 128 : (g + 1) * 128] for g in range(G)], axis=0)
        total = total + dot(left, n_ref[b].reshape(G * T, WIDE), TN)
    dwt = jnp.zeros((H, CP), F32)
    for i in range(I8):
        dwt = dwt + total[i * H : (i + 1) * H, i * CP : (i + 1) * CP]
    side = jnp.concatenate([dwt[0:8], dwt[8:16]], axis=1)
    for h in range(H):
        for half in range(2):
            at = (2 * h + half) * 16
            piece = jnp.concatenate([side, queries[at : at + 16]], axis=0)
            send_ref[half * PEERS + h] = piece.astype(BF16)
    for store in stores:
        store.wait()


def grads_kernel(side_ref, four_ref, w_ref, q_ref, g_ref, keep_ref, give_ref, all_ref):
    lanes = jnp.where(iota((T, HC), 0) == four_query((T, HC), 1), 1.0, 0.0).astype(BF16)
    row_head = (iota((HC, HC), 0) * 171) >> 12
    mask = (row_head & 3) == (iota((HC, HC), 1) & 3)

    def select(source):
        return jnp.where(mask, dot(source, lanes, TN), 0.0).astype(BF16)

    def gather(left, fours):
        quarter = HC // 4
        return jnp.concatenate(
            [dot(left[q * quarter : (q + 1) * quarter], fours[q], NT) for q in range(4)], axis=0
        )

    keys, values = [], []
    for b in range(B):
        keys.append(gather(select(q_ref[b]), [four_ref[b, q] for q in range(4)]) * SCALE)
        parts = [w_ref[b, :, g * 128 : (g + 1) * 128].astype(F32) for g in range(G)]
        values.append(gather(select(g_ref[b]), [four_heads(parts, q) for q in range(4)]))
    kv = jnp.concatenate(keys + values, axis=1)
    for h in range(H):
        for t in range(3):
            all_ref[h, t * C : (t + 1) * C, :] = kv[h * C : (h + 1) * C, t * 128 : (t + 1) * 128]
    y_lo = side_ref[0]
    for z in range(DEPTH):
        keep_ref[z] = all_ref[2 * z + y_lo].astype(BF16)
        give_ref[z] = all_ref[2 * z + 1 - y_lo].astype(BF16)


def pair_kernel(groups, scaled_ref, along_ref, n_ref, wt_ref, _, out_ref, ones_ref, diag_ref):
    first = pl.program_id(0) == 0

    @pl.when(first)
    def _():
        ones_ref[...] = block_diagonal(jnp.ones((128, CP), F32), H).astype(BF16)
        wt = wt_ref[...].astype(F32)
        wt = wt - jnp.mean(wt, axis=1, keepdims=True)
        diag_ref[...] = block_diagonal(jnp.concatenate([wt] * I8, axis=0), H).astype(BF16)

    rows = groups * T
    scaled = scaled_ref[0].reshape(rows, 128)
    along = along_ref[0].reshape(rows, 128)
    for p in range(I8 // 2):
        at = slice(p * 256, (p + 1) * 256)
        back = dot(scaled, diag_ref[:, at])
        normed = n_ref[0, :, :, at].reshape(rows, 256).astype(F32)
        grad = (back - normed * dot(along, ones_ref[:, at])).astype(BF16)
        for g in range(groups):
            for k in range(2):
                out_ref[0, g * I8 + 2 * p + k] = grad[g * T : (g + 1) * T, k * CP : (k + 1) * CP]


def bias_out_kernel(side_ref, got_ref, keep_ref, more_ref, _, send_ref, own_ref, other_ref):
    side = jnp.sum(got_ref[:, 0:8, :].astype(F32), axis=0)
    dwt = jnp.concatenate([side[:, :CP], side[:, CP:]], axis=0)
    for z in range(DEPTH):
        kv = keep_ref[z].astype(F32) + more_ref[z].astype(F32)
        send_ref[z] = jnp.concatenate([kv, dwt], axis=0).astype(BF16)
    parts = [
        jnp.sum(got_ref[y * PEERS : (y + 1) * PEERS, 8:24, :].astype(F32), axis=0) for y in range(2)
    ]
    first = side_ref[0] == 0
    own_ref[...] = jnp.where(first, parts[0], parts[1])
    other_ref[...] = jnp.where(first, parts[1], parts[0])


def queries_out_kernel(side_ref, own_ref, other_ref, query_ref):
    first = side_ref[0] == 0
    own, other = own_ref[0:12], other_ref[0:12]
    both = jnp.concatenate([jnp.where(first, own, other), jnp.where(first, other, own)], axis=0)
    for b in range(B):
        query_ref[b] = both[:, b * T : (b + 1) * T]


def keys_out_kernel(got_ref, key_ref, value_ref, dwt_ref):
    total = jnp.sum(got_ref[...].astype(F32), axis=0)
    kv = jnp.concatenate([total[t * C : (t + 1) * C] for t in range(3)], axis=1)
    for b in range(B):
        key_ref[b] = kv[:, b * T : (b + 1) * T]
        value_ref[b] = kv[:, (B + b) * T : (B + b + 1) * T]
    dwt_ref[...] = total[3 * C :]


def call(kernel, outs, limit, flops=0, moved=0, **kw):
    return pl.pallas_call(
        kernel,
        out_shape=outs,
        compiler_params=pltpu.CompilerParams(vmem_limit_bytes=limit << 20),
        cost_estimate=pl.CostEstimate(flops=flops, bytes_accessed=moved, transcendentals=0),
        **kw,
    )


def f32(*shape):
    return jax.ShapeDtypeStruct(shape, F32)


def bf16(*shape):
    return jax.ShapeDtypeStruct(shape, BF16)


def far(*shape):
    return pltpu.HBM(shape, BF16)


def in_hbm(x):
    return pltpu.with_memory_space_constraint(x, pltpu.HBM)


def expanded(query, grad):
    shape = bf16(B, HC, QH)
    outs = [shape, shape, bf16(256, B * HC), bf16(2 * H * 16, HC)]
    return call(expand_kernel, outs, 16, flops=400_000_000, moved=5_000_000)(query, grad)


def norm(pair, wt):
    groups = GROUPS
    spec = lambda *tail: pl.BlockSpec((1, groups, T) + tail, lambda b, s: (b, s, 0, 0))
    return call(
        lambda *refs: norm_kernel(groups, *refs),
        [far(B, G, T, WIDE), f32(B, G, T, 128), f32(B, G, T, 128)],
        24,
        flops=4_000_000_000,
        moved=12_000_000,
        grid=(B, G // groups),
        in_specs=[
            pl.BlockSpec((1, groups * I8, T, CP), lambda b, s: (b, s, 0, 0)),
            pl.BlockSpec((H, CP), lambda b, s: (0, 0)),
        ],
        out_specs=[spec(WIDE), spec(128), spec(128)],
        scratch_shapes=[pltpu.VMEM((256, 256), BF16), pltpu.VMEM((128, WIDE), BF16)],
    )(in_hbm(pair), in_hbm(wt))


def logits(k, v, qt, gt, bias):
    big = f32(B, G, T, 128)
    return call(
        logits_kernel, [big, big, f32(PEERS, 4 * G, 128)], 16, flops=1_000_000_000, moved=8_000_000
    )(k, v, qt, gt, bias)


def scores(*args):
    low = far(B, T, QH)
    four = far(B, 4, T, HC)
    cell = far(B, G, T, 128)
    whole = pl.BlockSpec(memory_space=pltpu.VMEM)
    hbm = pl.BlockSpec(memory_space=pltpu.HBM)
    return call(
        scores_kernel,
        [four, low, cell, cell, bf16(PLANE, 24, 256)],
        24,
        flops=2_500_000_000,
        moved=8_000_000,
        in_specs=[whole] * 9,
        out_specs=[hbm] * 4 + [whole],
        scratch_shapes=[
            pltpu.VMEM((B, T, QH), BF16),
            pltpu.VMEM((B, 4, T, HC), BF16),
            pltpu.VMEM((B, T, QH), BF16),
            pltpu.VMEM((B, G, T, 128), BF16),
            pltpu.VMEM((B, G, T, 128), BF16),
            pltpu.SemaphoreType.DMA((4,)),
        ],
    )(*args)


WHOLE = pl.BlockSpec(memory_space=pltpu.VMEM)
SCALAR = pl.BlockSpec(memory_space=pltpu.SMEM)


def grads(side, *args):
    half = bf16(DEPTH, 3 * C, 128)
    return call(
        grads_kernel,
        [half, half],
        24,
        flops=2_500_000_000,
        moved=8_000_000,
        in_specs=[SCALAR] + [WHOLE] * 4,
        scratch_shapes=[pltpu.VMEM((H, 3 * C, 128), F32)],
    )(side, *[in_hbm(x) for x in args])


def pair_grad(b, scaled, along, n, wt, done):
    groups = GROUPS
    spec = lambda *tail: pl.BlockSpec((1, groups, T) + tail, lambda s: (b, s, 0, 0))
    fresh = done is None
    return call(
        lambda *refs: pair_kernel(groups, *(refs if not fresh else refs[:4] + (None,) + refs[4:])),
        [far(B, T, T, CP)],
        24,
        flops=2_000_000_000,
        moved=5_000_000,
        grid=(G // groups,),
        in_specs=[spec(128), spec(128), spec(WIDE), pl.BlockSpec((H, CP), lambda s: (0, 0))]
        + ([] if fresh else [pl.BlockSpec(memory_space=pltpu.HBM)]),
        out_specs=[pl.BlockSpec((1, groups * I8, T, CP), lambda s: (b, s, 0, 0))],
        scratch_shapes=[pltpu.VMEM((128, WIDE), BF16), pltpu.VMEM((128, WIDE), BF16)],
        **({} if fresh else dict(input_output_aliases={4: 0})),
    )(in_hbm(scaled), in_hbm(along), in_hbm(n), in_hbm(wt), *([] if fresh else [done]))[0]


def bias_out(side, got, keep, more, after):
    half = f32(16, 256)
    return call(
        bias_out_kernel,
        [bf16(DEPTH, 3 * C + H, 128), half, half],
        16,
        in_specs=[SCALAR] + [WHOLE] * 3 + [pl.BlockSpec(memory_space=pltpu.HBM)],
    )(side, got, keep, more, in_hbm(after))


def queries_out(side, own, other):
    return call(queries_out_kernel, [f32(B, C, T)], 16, in_specs=[SCALAR] + [WHOLE] * 2)(
        side, own, other
    )[0]


def keys_out(got):
    half = f32(B, C, T)
    return call(keys_out_kernel, [half, half, f32(H, CP)], 16)(got)


ROUTE = (
    "58b92a73e4d1c60f",
    "1986b504d32cf7ea",
    "db0a9542736e1f8c",
    "a8b163d74e5fc290",
    "0a71fcdbe6498253",
    "f32ecda57b861940",
    "352c1def8b6a9704",
    "745d0cfe28196a3b",
    "c695e478103f2adb",
    "d54a9762b1e0f38c",
    "f986a704c523d1eb",
    "eb7d48910263ac5f",
    "16fe0ad982bc5437",
    "73e01fc859ab462d",
    "f1253da0cb84e976",
    "c039e21bfad54876",
)


def key_route():
    return [
        (col * PEERS + k, int(digit, 16) * PEERS + col)
        for col, line in enumerate(ROUTE)
        for k, digit in enumerate(line)
    ]


def spread_over(x, axis, groups=None):
    return lax.all_to_all(x, axis, 0, 0, tiled=True, axis_index_groups=groups)


def swap_y(x):
    return lax.ppermute(x, "row", [(r, r ^ 1) for r in range(PEERS)])


def shards(query_in, key_in, value_in, pair, bias_weight, d_out):
    route = key_route()
    k = lax.ppermute(key_in, ("row", "col"), route)
    v = lax.ppermute(value_in, ("row", "col"), route)
    wt = bias_weight.T
    side = (lax.axis_index("row") & 1).astype(jnp.int32).reshape(1)
    qt, gt, pick, turn = expanded(query_in, d_out)
    side, qt = lax.optimization_barrier((side, qt))
    n, bias, inv = norm(pair, wt)
    scaled_scores, dw, stats = logits(k, v, qt, gt, bias)
    stats = spread_over(stats, "col")
    ds, w, scaled, along, send = scores(
        stats, scaled_scores, dw, bias, inv, k, pick, turn, n
    )
    planes = [list(range(z * PLANE, (z + 1) * PLANE)) for z in range(DEPTH)]
    got = spread_over(send, ("row", "col"), planes)
    keep, give = grads(side, ds, w, query_in, d_out)
    d_pair = pair_grad(0, scaled, along, n, wt, None)
    send, own, other = bias_out(side, got, keep, swap_y(give), d_pair)
    lines = [list(range(y, PEERS, 2)) for y in range(2)]
    got = spread_over(send, "row", lines)
    d_query = queries_out(side, own, swap_y(other))
    d_pair = pair_grad(1, scaled, along, n, wt, d_pair)
    d_key, d_value, dwt = keys_out(got)
    flip = lambda x: jnp.swapaxes(x, 1, 2)
    return flip(d_query), flip(d_key), flip(d_value), d_pair, dwt.T


def solution(mesh):
    rows = P(None, "row", None)
    tiles = P(None, "row", "col", None)
    in_specs = (rows, rows, rows, tiles, P(), rows)
    swapped = P(None, "col", "row")
    out_specs = (P(None, "row", "col"), swapped, swapped, tiles, P())
    return jax.shard_map(shards, mesh=mesh, in_specs=in_specs, out_specs=out_specs, check_vma=False)
```

```python
import math

import jax
import jax.numpy as jnp
from jax import lax
from jax.experimental import pallas as pl
from jax.experimental.pallas import tpu as pltpu
from jax.sharding import PartitionSpec as P

EPS = 1e-05
F32 = jnp.float32
BF16 = jnp.bfloat16

B = 2
H = 16
C = 24
HC = H * C
CP = 128
T = 96
G = 12
I8 = 8
WIDE = I8 * CP
QH = T * H
SCALE = 1.0 / math.sqrt(C)
PEERS = 16
PLANE = 2 * PEERS
DEPTH = 8
GROUPS = 6

NN = (((1,), (0,)), ((), ()))
NT = (((1,), (1,)), ((), ()))
TN = (((0,), (0,)), ((), ()))


def dot(left, right, dims=NN):
    return lax.dot_general(left, right, dims, preferred_element_type=F32)


def iota(shape, dim):
    return lax.broadcasted_iota(jnp.int32, shape, dim)


def head_mask():
    row_head = (iota((HC, 128), 0) * 171) >> 12
    return row_head == (iota((HC, 128), 1) & (H - 1))


def query_lanes(rows, first):
    return jnp.where(iota((rows, QH), 0) - first == (iota((rows, QH), 1) >> 4), 1.0, 0.0).astype(BF16)


def block_diagonal(tile, rows_per_block):
    row_block = iota((128, CP), 0) // rows_per_block
    zero = jnp.zeros_like(tile)
    return jnp.concatenate([jnp.where(row_block == i, tile, zero) for i in range(I8)], axis=1)


def expand(source, target):
    lanes = query_lanes(T, 0)
    mask = head_mask()
    for b in range(B):
        spread = dot(source[b], lanes, TN)
        for g in range(G):
            at = slice(g * 128, (g + 1) * 128)
            target[b, :, at] = jnp.where(mask, spread[:, at], 0.0).astype(BF16)


def expand_kernel(q_ref, g_ref, qt_ref, gt_ref, pick_ref, turn_ref):
    expand(q_ref, qt_ref)
    expand(g_ref, gt_ref)
    lane = iota((256, B * HC), 1)
    batch = jnp.where(lane >= HC, 1, 0)
    within = lane - batch * HC
    query = (within >> 7) * 32 + (within >> 2 & 3) * I8 + (within >> 4 & 7)
    pick_ref[...] = jnp.where(iota((256, B * HC), 0) == batch * T + query, 1.0, 0.0).astype(BF16)
    row = iota((2 * H * 16, HC), 0)
    feature = (row >> 5) * C + (row >> 4 & 1) * 12 + (row & 15)
    used = ((row & 15) < 12) & (iota((2 * H * 16, HC), 1) == feature)
    turn_ref[...] = jnp.where(used, 1.0, 0.0).astype(BF16)


def norm_kernel(
    groups, pair_ref, wt_ref, n_ref, bias_ref, low_bias_ref, inv_ref, ones_ref, diag_ref
):
    first = (pl.program_id(0) == 0) & (pl.program_id(1) == 0)

    @pl.when(first)
    def _():
        same = (iota((256, 256), 0) >> 7) == (iota((256, 256), 1) >> 7)
        ones_ref[...] = jnp.where(same, 1.0 / CP, 0.0).astype(BF16)
        wt = wt_ref[...].astype(F32)
        diag_ref[...] = block_diagonal(jnp.concatenate([wt] * I8, axis=0), H).astype(BF16)

    ones = ones_ref[...]
    rows = groups * T
    lane_query = iota((rows, 128), 1) >> 4
    compact = jnp.zeros((rows, 128), F32)
    bias = jnp.zeros((rows, 128), F32)
    for p in range(I8 // 2):
        x = jnp.concatenate(
            [
                jnp.concatenate([pair_ref[0, g * I8 + 2 * p], pair_ref[0, g * I8 + 2 * p + 1]], axis=1)
                for g in range(groups)
            ],
            axis=0,
        )
        centred = x.astype(F32) - dot(x, ones)
        spread = dot((centred * centred).astype(BF16), ones)
        inverse = lax.rsqrt(spread + EPS)
        normed = (centred * inverse).astype(BF16)
        n_ref[0, :, :, p * 256 : (p + 1) * 256] = normed.reshape(groups, T, 256)
        for k in range(2):
            compact = jnp.where(
                lane_query == 2 * p + k, inverse[:, k * CP : (k + 1) * CP], compact
            )
        bias = bias + dot(normed, diag_ref[:, p * 256 : (p + 1) * 256], NT)
    inv_ref[0] = compact.reshape(groups, T, 128).astype(BF16)
    bias = bias.reshape(groups, T, 128)
    bias_ref[0] = bias
    low_bias_ref[0] = (bias * (1.0 / CP)).astype(BF16)


def logits_kernel(k_ref, v_ref, qt_ref, gt_ref, bias_ref, logits_ref, dw_ref, stats_ref):
    for b in range(B):
        scores = dot(k_ref[b], qt_ref[b])
        inner = dot(v_ref[b], gt_ref[b])
        for g in range(G):
            at = slice(g * 128, (g + 1) * 128)
            logits = scores[:, at] * SCALE + bias_ref[b, g]
            dw = inner[:, at]
            logits_ref[b, g] = logits
            dw_ref[b, g] = dw
            top = jnp.max(logits, axis=0, keepdims=True)
            expo = jnp.exp(logits - top)
            total = jnp.sum(expo, axis=0, keepdims=True)
            level = top + jnp.log(total)
            balance = jnp.sum(expo * dw, axis=0, keepdims=True) / total
            row = b * 2 * G + g
            stats_ref[:, row : row + 1, :] = jnp.broadcast_to(level[None], (PEERS, 1, 128))
            stats_ref[:, row + G : row + G + 1, :] = jnp.broadcast_to(balance[None], (PEERS, 1, 128))


def four_query(shape, dim):
    lane = iota(shape, dim)
    return (lane >> 7) * 32 + (lane >> 2 & 3) * I8 + (lane >> 4 & 7)


def four_heads(parts, q):
    slot = iota((T, 128), 1) >> 2 & 3
    tiles = []
    for wide in range(G // 4):
        tile = parts[wide * 4 + q]
        for k in range(4):
            if k != q:
                moved = pltpu.roll(parts[wide * 4 + k], (4 * (k - q)) % 128, 1)
                tile = jnp.where(slot == k, moved, tile)
        tiles.append(tile.astype(BF16))
    return jnp.concatenate(tiles, axis=1)


def scores_kernel(
    stats_ref, logits_ref, dw_ref, k_ref, pick_ref, turn_ref, n_ref,
    four_out, w_out, ds_out, send_ref,
    ds_ref, four_ref, w_ref, sems,
):
    keep = iota((128, HC), 0) >> 5 == (iota((128, HC), 1) & 3)
    pairs = ((four_ref, four_out), (w_ref, w_out), (ds_ref, ds_out))
    stores = []
    for b in range(B):
        levels = stats_ref[:, b * 2 * G : b * 2 * G + G, :]
        balances = stats_ref[:, b * 2 * G + G : (b + 1) * 2 * G, :]
        top = jnp.max(levels, axis=0)
        parts = jnp.exp(levels - top[None])
        total = jnp.sum(parts, axis=0)
        level = top + jnp.log(total)
        balance = jnp.sum(parts * balances, axis=0) / total
        lows = []
        for g in range(G):
            weights = jnp.exp(logits_ref[b, g] - level[g : g + 1])
            low = (weights * (dw_ref[b, g] - balance[g : g + 1])).astype(BF16)
            ds_ref[b, g] = low
            w_ref[b, g] = weights.astype(BF16)
            lows.append(low.astype(F32))
        for q in range(4):
            four_ref[b, q] = four_heads(lows, q)
        for i, (x, y) in enumerate(pairs):
            store = pltpu.make_async_copy(x.at[b], y.at[b], sems.at[b * 3 + i])
            store.start()
            stores.append(store)

    chosen = []
    for b in range(B):
        k_turned = dot(turn_ref[...], k_ref[b], NT).astype(BF16)
        quarters = []
        for q in range(4):
            spread = dot(k_turned[q * 128 : (q + 1) * 128], four_ref[b, q])
            quarters.append(jnp.where(keep, spread, 0.0).astype(BF16))
        chosen.append(jnp.concatenate(quarters, axis=0))
    queries = dot(jnp.concatenate(chosen, axis=1), pick_ref[...], NT) * SCALE

    total = jnp.zeros((128, WIDE), F32)
    for b in range(B):
        total = total + dot(ds_ref[b].reshape(G * T, 128), n_ref[b].reshape(G * T, WIDE), TN)
    dwt = jnp.zeros((H, CP), F32)
    for i in range(I8):
        dwt = dwt + total[i * H : (i + 1) * H, i * CP : (i + 1) * CP]
    side = jnp.concatenate([dwt[0:8], dwt[8:16]], axis=1)
    for h in range(H):
        for half in range(2):
            at = (2 * h + half) * 16
            piece = jnp.concatenate([side, queries[at : at + 16]], axis=0)
            send_ref[half * PEERS + h] = piece.astype(BF16)
    for store in stores:
        store.wait()


def grads_kernel(side_ref, four_ref, w_ref, q_ref, g_ref, keep_ref, give_ref, all_ref):
    lanes = jnp.where(iota((T, HC), 0) == four_query((T, HC), 1), 1.0, 0.0).astype(BF16)
    row_head = (iota((HC, HC), 0) * 171) >> 12
    mask = (row_head & 3) == (iota((HC, HC), 1) & 3)

    def select(source):
        return jnp.where(mask, dot(source, lanes, TN), 0.0).astype(BF16)

    def gather(left, fours):
        quarter = HC // 4
        return jnp.concatenate(
            [dot(left[q * quarter : (q + 1) * quarter], fours[q], NT) for q in range(4)], axis=0
        )

    keys, values = [], []
    for b in range(B):
        keys.append(gather(select(q_ref[b]), [four_ref[b, q] for q in range(4)]) * SCALE)
        parts = [w_ref[b, g].astype(F32) for g in range(G)]
        values.append(gather(select(g_ref[b]), [four_heads(parts, q) for q in range(4)]))
    kv = jnp.concatenate(keys + values, axis=1)
    for h in range(H):
        for t in range(3):
            all_ref[h, t * C : (t + 1) * C, :] = kv[h * C : (h + 1) * C, t * 128 : (t + 1) * 128]
    y_lo = side_ref[0]
    for z in range(DEPTH):
        keep_ref[z] = all_ref[2 * z + y_lo].astype(BF16)
        give_ref[z] = all_ref[2 * z + 1 - y_lo].astype(BF16)


def pair_kernel(
    groups, ds_ref, inv_ref, bias_ref, n_ref, wt_ref, _, out_ref, ones_ref, diag_ref
):
    first = pl.program_id(0) == 0

    @pl.when(first)
    def _():
        ones_ref[...] = block_diagonal(jnp.ones((128, CP), F32), H).astype(BF16)
        wt = wt_ref[...].astype(F32)
        wt = wt - jnp.mean(wt, axis=1, keepdims=True)
        diag_ref[...] = block_diagonal(jnp.concatenate([wt] * I8, axis=0), H).astype(BF16)

    rows = groups * T
    scaled = ds_ref[0].astype(F32) * inv_ref[0].astype(F32)
    along = (scaled * bias_ref[0].astype(F32)).astype(BF16).reshape(rows, 128)
    scaled = scaled.astype(BF16).reshape(rows, 128)
    for p in range(I8 // 2):
        at = slice(p * 256, (p + 1) * 256)
        back = dot(scaled, diag_ref[:, at])
        normed = n_ref[0, :, :, at].reshape(rows, 256).astype(F32)
        grad = (back - normed * dot(along, ones_ref[:, at])).astype(BF16)
        for g in range(groups):
            for k in range(2):
                out_ref[0, g * I8 + 2 * p + k] = grad[g * T : (g + 1) * T, k * CP : (k + 1) * CP]


def bias_out_kernel(side_ref, got_ref, keep_ref, more_ref, _, send_ref, own_ref, other_ref):
    side = jnp.sum(got_ref[:, 0:8, :].astype(F32), axis=0)
    dwt = jnp.concatenate([side[:, :CP], side[:, CP:]], axis=0)
    for z in range(DEPTH):
        kv = keep_ref[z].astype(F32) + more_ref[z].astype(F32)
        send_ref[z] = jnp.concatenate([kv, dwt], axis=0).astype(BF16)
    parts = [
        jnp.sum(got_ref[y * PEERS : (y + 1) * PEERS, 8:24, :].astype(F32), axis=0) for y in range(2)
    ]
    first = side_ref[0] == 0
    own_ref[...] = jnp.where(first, parts[0], parts[1])
    other_ref[...] = jnp.where(first, parts[1], parts[0])


def queries_out_kernel(side_ref, own_ref, other_ref, query_ref):
    first = side_ref[0] == 0
    own, other = own_ref[0:12], other_ref[0:12]
    both = jnp.concatenate([jnp.where(first, own, other), jnp.where(first, other, own)], axis=0)
    for b in range(B):
        query_ref[b] = both[:, b * T : (b + 1) * T]


def keys_out_kernel(got_ref, key_ref, value_ref, dwt_ref):
    total = jnp.sum(got_ref[...].astype(F32), axis=0)
    kv = jnp.concatenate([total[t * C : (t + 1) * C] for t in range(3)], axis=1)
    for b in range(B):
        key_ref[b] = kv[:, b * T : (b + 1) * T]
        value_ref[b] = kv[:, (B + b) * T : (B + b + 1) * T]
    dwt_ref[...] = total[3 * C :]


def call(kernel, outs, limit, flops=0, moved=0, **kw):
    return pl.pallas_call(
        kernel,
        out_shape=outs,
        compiler_params=pltpu.CompilerParams(vmem_limit_bytes=limit << 20),
        cost_estimate=pl.CostEstimate(flops=flops, bytes_accessed=moved, transcendentals=0),
        **kw,
    )


def f32(*shape):
    return jax.ShapeDtypeStruct(shape, F32)


def bf16(*shape):
    return jax.ShapeDtypeStruct(shape, BF16)


def far(*shape):
    return pltpu.HBM(shape, BF16)


def in_hbm(x):
    return pltpu.with_memory_space_constraint(x, pltpu.HBM)


WHOLE = pl.BlockSpec(memory_space=pltpu.VMEM)
SCALAR = pl.BlockSpec(memory_space=pltpu.SMEM)


def expanded(query, grad):
    shape = bf16(B, HC, QH)
    outs = [shape, shape, bf16(256, B * HC), bf16(2 * H * 16, HC)]
    return call(expand_kernel, outs, 16, flops=400_000_000, moved=5_000_000)(query, grad)


def norm(pair, wt):
    groups = GROUPS
    spec = lambda *tail: pl.BlockSpec((1, groups, T) + tail, lambda b, s: (b, s, 0, 0))
    return call(
        lambda *refs: norm_kernel(groups, *refs),
        [far(B, G, T, WIDE), f32(B, G, T, 128), far(B, G, T, 128), far(B, G, T, 128)],
        24,
        flops=4_000_000_000,
        moved=12_000_000,
        grid=(B, G // groups),
        in_specs=[
            pl.BlockSpec((1, groups * I8, T, CP), lambda b, s: (b, s, 0, 0)),
            pl.BlockSpec((H, CP), lambda b, s: (0, 0)),
        ],
        out_specs=[spec(WIDE), spec(128), spec(128), spec(128)],
        scratch_shapes=[pltpu.VMEM((256, 256), BF16), pltpu.VMEM((128, WIDE), BF16)],
    )(in_hbm(pair), in_hbm(wt))


def logits(k, v, qt, gt, bias):
    big = f32(B, G, T, 128)
    return call(
        logits_kernel, [big, big, f32(PEERS, 4 * G, 128)], 16, flops=1_000_000_000, moved=8_000_000
    )(k, v, qt, gt, bias)


def scores(*args):
    cell = far(B, G, T, 128)
    hbm = pl.BlockSpec(memory_space=pltpu.HBM)
    return call(
        scores_kernel,
        [far(B, 4, T, HC), cell, cell, bf16(PLANE, 24, 256)],
        24,
        flops=2_500_000_000,
        moved=8_000_000,
        in_specs=[WHOLE] * 7,
        out_specs=[hbm] * 3 + [WHOLE],
        scratch_shapes=[
            pltpu.VMEM((B, G, T, 128), BF16),
            pltpu.VMEM((B, 4, T, HC), BF16),
            pltpu.VMEM((B, G, T, 128), BF16),
            pltpu.SemaphoreType.DMA((3 * B,)),
        ],
    )(*args)


def grads(side, *args):
    half = bf16(DEPTH, 3 * C, 128)
    return call(
        grads_kernel,
        [half, half],
        24,
        flops=2_500_000_000,
        moved=8_000_000,
        in_specs=[SCALAR] + [WHOLE] * 4,
        scratch_shapes=[pltpu.VMEM((H, 3 * C, 128), F32)],
    )(side, *[in_hbm(x) for x in args])


def pair_grad(b, ds, inv, bias, n, wt, done):
    groups = GROUPS
    spec = lambda *tail: pl.BlockSpec((1, groups, T) + tail, lambda s: (b, s, 0, 0))
    fresh = done is None
    return call(
        lambda *refs: pair_kernel(groups, *(refs if not fresh else refs[:5] + (None,) + refs[5:])),
        [far(B, T, T, CP)],
        24,
        flops=2_000_000_000,
        moved=5_000_000,
        grid=(G // groups,),
        in_specs=[spec(128)] * 3 + [spec(WIDE), pl.BlockSpec((H, CP), lambda s: (0, 0))]
        + ([] if fresh else [pl.BlockSpec(memory_space=pltpu.HBM)]),
        out_specs=[pl.BlockSpec((1, groups * I8, T, CP), lambda s: (b, s, 0, 0))],
        scratch_shapes=[pltpu.VMEM((128, WIDE), BF16), pltpu.VMEM((128, WIDE), BF16)],
        **({} if fresh else dict(input_output_aliases={5: 0})),
    )(*[in_hbm(x) for x in (ds, inv, bias, n, wt)], *([] if fresh else [done]))[0]


def bias_out(side, got, keep, more, after):
    half = f32(16, 256)
    return call(
        bias_out_kernel,
        [bf16(DEPTH, 3 * C + H, 128), half, half],
        16,
        in_specs=[SCALAR] + [WHOLE] * 3 + [pl.BlockSpec(memory_space=pltpu.HBM)],
    )(side, got, keep, more, in_hbm(after))


def queries_out(side, own, other):
    return call(queries_out_kernel, [f32(B, C, T)], 16, in_specs=[SCALAR] + [WHOLE] * 2)(
        side, own, other
    )[0]


def keys_out(got):
    half = f32(B, C, T)
    return call(keys_out_kernel, [half, half, f32(H, CP)], 16)(got)


ROUTE = (
    "58b92a73e4d1c60f",
    "1986b504d32cf7ea",
    "db0a9542736e1f8c",
    "a8b163d74e5fc290",
    "0a71fcdbe6498253",
    "f32ecda57b861940",
    "352c1def8b6a9704",
    "745d0cfe28196a3b",
    "c695e478103f2adb",
    "d54a9762b1e0f38c",
    "f986a704c523d1eb",
    "eb7d48910263ac5f",
    "16fe0ad982bc5437",
    "73e01fc859ab462d",
    "f1253da0cb84e976",
    "c039e21bfad54876",
)


def key_route():
    return [
        (col * PEERS + k, int(digit, 16) * PEERS + col)
        for col, line in enumerate(ROUTE)
        for k, digit in enumerate(line)
    ]


def spread_over(x, axis, groups=None):
    return lax.all_to_all(x, axis, 0, 0, tiled=True, axis_index_groups=groups)


def swap_y(x):
    return lax.ppermute(x, "row", [(r, r ^ 1) for r in range(PEERS)])


def shards(query_in, key_in, value_in, pair, bias_weight, d_out):
    route = key_route()
    k = lax.ppermute(key_in, ("row", "col"), route)
    v = lax.ppermute(value_in, ("row", "col"), route)
    wt = bias_weight.T
    side = (lax.axis_index("row") & 1).astype(jnp.int32).reshape(1)
    qt, gt, pick, turn = expanded(query_in, d_out)
    side, qt = lax.optimization_barrier((side, qt))
    n, bias, low_bias, inv = norm(pair, wt)
    scaled_scores, dw, stats = logits(k, v, qt, gt, bias)
    stats = spread_over(stats, "col")
    four, w, ds, send = scores(stats, scaled_scores, dw, k, pick, turn, n)
    planes = [list(range(z * PLANE, (z + 1) * PLANE)) for z in range(DEPTH)]
    got = spread_over(send, ("row", "col"), planes)
    keep, give = grads(side, four, w, query_in, d_out)
    d_pair = pair_grad(0, ds, inv, low_bias, n, wt, None)
    send, own, other = bias_out(side, got, keep, swap_y(give), d_pair)
    lines = [list(range(y, PEERS, 2)) for y in range(2)]
    got = spread_over(send, "row", lines)
    d_query = queries_out(side, own, swap_y(other))
    d_pair = pair_grad(1, ds, inv, low_bias, n, wt, d_pair)
    d_key, d_value, dwt = keys_out(got)
    flip = lambda x: jnp.swapaxes(x, 1, 2)
    return flip(d_query), flip(d_key), flip(d_value), d_pair, dwt.T


def solution(mesh):
    rows = P(None, "row", None)
    tiles = P(None, "row", "col", None)
    in_specs = (rows, rows, rows, tiles, P(), rows)
    swapped = P(None, "col", "row")
    out_specs = (P(None, "row", "col"), swapped, swapped, tiles, P())
    return jax.shard_map(shards, mesh=mesh, in_specs=in_specs, out_specs=out_specs, check_vma=False)
```

```python
import math

import jax
import jax.numpy as jnp
from jax import lax
from jax.experimental import pallas as pl
from jax.experimental.pallas import tpu as pltpu
from jax.sharding import PartitionSpec as P

EPS = 1e-05
F32 = jnp.float32
BF16 = jnp.bfloat16

B = 2
H = 16
C = 24
HC = H * C
CP = 128
T = 96
G = 12
I8 = 8
WIDE = I8 * CP
QH = T * H
SCALE = 1.0 / math.sqrt(C)
PEERS = 16
PLANE = 2 * PEERS
DEPTH = 8
GROUPS = 6

NN = (((1,), (0,)), ((), ()))
NT = (((1,), (1,)), ((), ()))
TN = (((0,), (0,)), ((), ()))


def dot(left, right, dims=NN):
    return lax.dot_general(left, right, dims, preferred_element_type=F32)


def iota(shape, dim):
    return lax.broadcasted_iota(jnp.int32, shape, dim)


def head_mask():
    row_head = (iota((HC, 128), 0) * 171) >> 12
    return row_head == (iota((HC, 128), 1) & (H - 1))


def query_lanes(rows, first):
    return jnp.where(iota((rows, QH), 0) - first == (iota((rows, QH), 1) >> 4), 1.0, 0.0).astype(BF16)


def block_diagonal(tile, rows_per_block):
    row_block = iota((128, CP), 0) // rows_per_block
    zero = jnp.zeros_like(tile)
    return jnp.concatenate([jnp.where(row_block == i, tile, zero) for i in range(I8)], axis=1)


def expand(source, target):
    lanes = query_lanes(T, 0)
    mask = head_mask()
    for b in range(B):
        spread = dot(source[b], lanes, TN)
        for g in range(G):
            at = slice(g * 128, (g + 1) * 128)
            target[b, :, at] = jnp.where(mask, spread[:, at], 0.0).astype(BF16)


def expand_kernel(q_ref, g_ref, qt_ref, gt_ref, pick_ref, turn_ref):
    expand(q_ref, qt_ref)
    expand(g_ref, gt_ref)
    lane = iota((256, B * HC), 1)
    batch = jnp.where(lane >= HC, 1, 0)
    within = lane - batch * HC
    query = (within >> 7) * 32 + (within >> 2 & 3) * I8 + (within >> 4 & 7)
    pick_ref[...] = jnp.where(iota((256, B * HC), 0) == batch * 128 + query, 1.0, 0.0).astype(BF16)
    turn_ref[...] = jnp.where(iota((HC, HC), 0) == iota((HC, HC), 1), 1.0, 0.0).astype(BF16)


def norm_kernel(
    groups, pair_ref, wt_ref, n_ref, bias_ref, low_bias_ref, inv_ref, ones_ref, diag_ref
):
    first = (pl.program_id(0) == 0) & (pl.program_id(1) == 0)

    @pl.when(first)
    def _():
        same = (iota((256, 256), 0) >> 7) == (iota((256, 256), 1) >> 7)
        ones_ref[...] = jnp.where(same, 1.0 / CP, 0.0).astype(BF16)
        wt = wt_ref[...].astype(F32)
        diag_ref[...] = block_diagonal(jnp.concatenate([wt] * I8, axis=0), H).astype(BF16)

    ones = ones_ref[...]
    rows = groups * T
    lane_query = iota((rows, 128), 1) >> 4
    compact = jnp.zeros((rows, 128), F32)
    bias = jnp.zeros((rows, 128), F32)
    for p in range(I8 // 2):
        x = jnp.concatenate(
            [
                jnp.concatenate([pair_ref[0, g * I8 + 2 * p], pair_ref[0, g * I8 + 2 * p + 1]], axis=1)
                for g in range(groups)
            ],
            axis=0,
        )
        wide = x.astype(F32)
        means = [
            jnp.mean(wide[:, k * CP : (k + 1) * CP], axis=1, keepdims=True) for k in range(2)
        ]
        centred = wide - jnp.concatenate([jnp.broadcast_to(m, (rows, CP)) for m in means], axis=1)
        spread = dot((centred * centred).astype(BF16), ones)
        inverse = lax.rsqrt(spread + EPS)
        normed = (centred * inverse).astype(BF16)
        n_ref[0, :, :, p * 256 : (p + 1) * 256] = normed.reshape(groups, T, 256)
        for k in range(2):
            compact = jnp.where(
                lane_query == 2 * p + k, inverse[:, k * CP : (k + 1) * CP], compact
            )
        bias = bias + dot(normed, diag_ref[:, p * 256 : (p + 1) * 256], NT)
    inv_ref[0] = compact.reshape(groups, T, 128).astype(BF16)
    bias = bias.reshape(groups, T, 128)
    bias_ref[0] = bias
    low_bias_ref[0] = (bias * (1.0 / CP)).astype(BF16)


def logits_kernel(k_ref, v_ref, qt_ref, gt_ref, bias_ref, logits_ref, dw_ref, stats_ref):
    for b in range(B):
        scores = dot(k_ref[b], qt_ref[b])
        inner = dot(v_ref[b], gt_ref[b])
        for g in range(G):
            at = slice(g * 128, (g + 1) * 128)
            logits = scores[:, at] * SCALE + bias_ref[b, g]
            dw = inner[:, at]
            logits_ref[b, g] = logits
            dw_ref[b, g] = dw
            top = jnp.max(logits, axis=0, keepdims=True)
            expo = jnp.exp(logits - top)
            total = jnp.sum(expo, axis=0, keepdims=True)
            level = top + jnp.log(total)
            balance = jnp.sum(expo * dw, axis=0, keepdims=True) / total
            row = b * 2 * G + g
            stats_ref[:, row : row + 1, :] = jnp.broadcast_to(level[None], (PEERS, 1, 128))
            stats_ref[:, row + G : row + G + 1, :] = jnp.broadcast_to(balance[None], (PEERS, 1, 128))


def four_query(shape, dim):
    lane = iota(shape, dim)
    return (lane >> 7) * 32 + (lane >> 2 & 3) * I8 + (lane >> 4 & 7)


def four_heads(parts, q):
    slot = iota((T, 128), 1) >> 2 & 3
    tiles = []
    for wide in range(G // 4):
        tile = parts[wide * 4 + q]
        for k in range(4):
            if k != q:
                moved = pltpu.roll(parts[wide * 4 + k], (4 * (k - q)) % 128, 1)
                tile = jnp.where(slot == k, moved, tile)
        tiles.append(tile.astype(BF16))
    return jnp.concatenate(tiles, axis=1)


def scores_kernel(
    stats_ref, logits_ref, dw_ref, k_ref, pick_ref, turn_ref, n_ref,
    four_out, w_out, ds_out, send_ref,
    ds_ref, four_ref, w_ref, sems,
):
    keep = (iota((HC // 4, HC), 0) * 171) >> 12 == (iota((HC // 4, HC), 1) & 3)
    pairs = ((four_ref, four_out), (w_ref, w_out), (ds_ref, ds_out))
    stores = []
    for b in range(B):
        levels = stats_ref[:, b * 2 * G : b * 2 * G + G, :]
        balances = stats_ref[:, b * 2 * G + G : (b + 1) * 2 * G, :]
        top = jnp.max(levels, axis=0)
        parts = jnp.exp(levels - top[None])
        total = jnp.sum(parts, axis=0)
        level = top + jnp.log(total)
        balance = jnp.sum(parts * balances, axis=0) / total
        lows = []
        for g in range(G):
            weights = jnp.exp(logits_ref[b, g] - level[g : g + 1])
            low = (weights * (dw_ref[b, g] - balance[g : g + 1])).astype(BF16)
            ds_ref[b, g] = low
            w_ref[b, g] = weights.astype(BF16)
            lows.append(low.astype(F32))
        for q in range(4):
            four_ref[b, q] = four_heads(lows, q)
        for i, (x, y) in enumerate(pairs):
            store = pltpu.make_async_copy(x.at[b], y.at[b], sems.at[b * 3 + i])
            store.start()
            stores.append(store)

    chosen = []
    for b in range(B):
        k_turned = dot(turn_ref[...], k_ref[b], NT).astype(BF16)
        quarters = []
        for q in range(4):
            spread = dot(k_turned[q * HC // 4 : (q + 1) * HC // 4], four_ref[b, q])
            quarters.append(jnp.where(keep, spread, 0.0).astype(BF16))
        chosen.append(jnp.concatenate(quarters, axis=0))
    queries = dot(jnp.concatenate(chosen, axis=1), pick_ref[...], NT) * SCALE

    total = jnp.zeros((128, WIDE), F32)
    for b in range(B):
        total = total + dot(ds_ref[b].reshape(G * T, 128), n_ref[b].reshape(G * T, WIDE), TN)
    dwt = jnp.zeros((H, CP), F32)
    for i in range(I8):
        dwt = dwt + total[i * H : (i + 1) * H, i * CP : (i + 1) * CP]
    for half in range(B):
        for h in range(H):
            own = queries[h * C : (h + 1) * C, half * 128 : (half + 1) * 128]
            send_ref[half * PEERS + h] = jnp.concatenate([own, dwt], axis=0).astype(BF16)
    for store in stores:
        store.wait()


def grads_kernel(side_ref, four_ref, w_ref, q_ref, g_ref, keep_ref, give_ref, all_ref):
    lanes = jnp.where(iota((T, HC), 0) == four_query((T, HC), 1), 1.0, 0.0).astype(BF16)
    row_head = (iota((HC, HC), 0) * 171) >> 12
    mask = (row_head & 3) == (iota((HC, HC), 1) & 3)

    def select(source):
        return jnp.where(mask, dot(source, lanes, TN), 0.0).astype(BF16)

    def gather(left, fours):
        quarter = HC // 4
        return jnp.concatenate(
            [dot(left[q * quarter : (q + 1) * quarter], fours[q], NT) for q in range(4)], axis=0
        )

    keys, values = [], []
    for b in range(B):
        keys.append(gather(select(q_ref[b]), [four_ref[b, q] for q in range(4)]) * SCALE)
        parts = [w_ref[b, g].astype(F32) for g in range(G)]
        values.append(gather(select(g_ref[b]), [four_heads(parts, q) for q in range(4)]))
    kv = jnp.concatenate(keys + values, axis=1)
    for h in range(H):
        for t in range(3):
            all_ref[h, t * C : (t + 1) * C, :] = kv[h * C : (h + 1) * C, t * 128 : (t + 1) * 128]
    y_lo = side_ref[0]
    for z in range(DEPTH):
        keep_ref[z] = all_ref[2 * z + y_lo].astype(BF16)
        give_ref[z] = all_ref[2 * z + 1 - y_lo].astype(BF16)


def pair_kernel(
    groups, ds_ref, inv_ref, bias_ref, n_ref, wt_ref, _, out_ref, ones_ref, diag_ref
):
    first = pl.program_id(0) == 0

    @pl.when(first)
    def _():
        ones_ref[...] = block_diagonal(jnp.ones((128, CP), F32), H).astype(BF16)
        wt = wt_ref[...].astype(F32)
        wt = wt - jnp.mean(wt, axis=1, keepdims=True)
        diag_ref[...] = block_diagonal(jnp.concatenate([wt] * I8, axis=0), H).astype(BF16)

    rows = groups * T
    scaled = ds_ref[0].astype(F32) * inv_ref[0].astype(F32)
    along = (scaled * bias_ref[0].astype(F32)).astype(BF16).reshape(rows, 128)
    scaled = scaled.astype(BF16).reshape(rows, 128)
    for p in range(I8 // 2):
        at = slice(p * 256, (p + 1) * 256)
        back = dot(scaled, diag_ref[:, at])
        normed = n_ref[0, :, :, at].reshape(rows, 256).astype(F32)
        grad = (back - normed * dot(along, ones_ref[:, at])).astype(BF16)
        for g in range(groups):
            for k in range(2):
                out_ref[0, g * I8 + 2 * p + k] = grad[g * T : (g + 1) * T, k * CP : (k + 1) * CP]


def bias_out_kernel(side_ref, got_ref, keep_ref, more_ref, _, send_ref, own_ref, other_ref):
    dwt = jnp.sum(got_ref[:, C : C + H, :].astype(F32), axis=0)
    for z in range(DEPTH):
        kv = keep_ref[z].astype(F32) + more_ref[z].astype(F32)
        send_ref[z] = jnp.concatenate([kv, dwt], axis=0).astype(BF16)
    parts = [
        jnp.sum(got_ref[y * PEERS : (y + 1) * PEERS, 0:C, :].astype(F32), axis=0) for y in range(2)
    ]
    first = side_ref[0] == 0
    own_ref[...] = jnp.where(first, parts[0], parts[1])
    other_ref[...] = jnp.where(first, parts[1], parts[0])


def queries_out_kernel(side_ref, own_ref, other_ref, query_ref):
    first = side_ref[0] == 0
    own, other = own_ref[:, 0:T], other_ref[:, 0:T]
    query_ref[0] = jnp.where(first, own, other)
    query_ref[1] = jnp.where(first, other, own)


def keys_out_kernel(got_ref, key_ref, value_ref, dwt_ref):
    total = jnp.sum(got_ref[...].astype(F32), axis=0)
    kv = jnp.concatenate([total[t * C : (t + 1) * C] for t in range(3)], axis=1)
    for b in range(B):
        key_ref[b] = kv[:, b * T : (b + 1) * T]
        value_ref[b] = kv[:, (B + b) * T : (B + b + 1) * T]
    dwt_ref[...] = total[3 * C :]


def call(kernel, outs, limit, flops=0, moved=0, **kw):
    return pl.pallas_call(
        kernel,
        out_shape=outs,
        compiler_params=pltpu.CompilerParams(vmem_limit_bytes=limit << 20),
        cost_estimate=pl.CostEstimate(flops=flops, bytes_accessed=moved, transcendentals=0),
        **kw,
    )


def f32(*shape):
    return jax.ShapeDtypeStruct(shape, F32)


def bf16(*shape):
    return jax.ShapeDtypeStruct(shape, BF16)


def far(*shape):
    return pltpu.HBM(shape, BF16)


def in_hbm(x):
    return pltpu.with_memory_space_constraint(x, pltpu.HBM)


WHOLE = pl.BlockSpec(memory_space=pltpu.VMEM)
SCALAR = pl.BlockSpec(memory_space=pltpu.SMEM)


def expanded(query, grad):
    shape = bf16(B, HC, QH)
    outs = [shape, shape, bf16(256, B * HC), bf16(HC, HC)]
    return call(expand_kernel, outs, 16, flops=400_000_000, moved=5_000_000)(query, grad)


def norm(pair, wt):
    groups = GROUPS
    spec = lambda *tail: pl.BlockSpec((1, groups, T) + tail, lambda b, s: (b, s, 0, 0))
    return call(
        lambda *refs: norm_kernel(groups, *refs),
        [far(B, G, T, WIDE), f32(B, G, T, 128), far(B, G, T, 128), far(B, G, T, 128)],
        24,
        flops=4_000_000_000,
        moved=12_000_000,
        grid=(B, G // groups),
        in_specs=[
            pl.BlockSpec((1, groups * I8, T, CP), lambda b, s: (b, s, 0, 0)),
            pl.BlockSpec((H, CP), lambda b, s: (0, 0)),
        ],
        out_specs=[spec(WIDE), spec(128), spec(128), spec(128)],
        scratch_shapes=[pltpu.VMEM((256, 256), BF16), pltpu.VMEM((128, WIDE), BF16)],
    )(in_hbm(pair), in_hbm(wt))


def logits(k, v, qt, gt, bias):
    big = f32(B, G, T, 128)
    return call(
        logits_kernel, [big, big, f32(PEERS, 4 * G, 128)], 16, flops=1_000_000_000, moved=8_000_000
    )(k, v, qt, gt, bias)


def scores(*args):
    cell = far(B, G, T, 128)
    hbm = pl.BlockSpec(memory_space=pltpu.HBM)
    return call(
        scores_kernel,
        [far(B, 4, T, HC), cell, cell, bf16(PLANE, C + H, 128)],
        24,
        flops=2_500_000_000,
        moved=8_000_000,
        in_specs=[WHOLE] * 7,
        out_specs=[hbm] * 3 + [WHOLE],
        scratch_shapes=[
            pltpu.VMEM((B, G, T, 128), BF16),
            pltpu.VMEM((B, 4, T, HC), BF16),
            pltpu.VMEM((B, G, T, 128), BF16),
            pltpu.SemaphoreType.DMA((3 * B,)),
        ],
    )(*args)


def grads(side, *args):
    half = bf16(DEPTH, 3 * C, 128)
    return call(
        grads_kernel,
        [half, half],
        24,
        flops=2_500_000_000,
        moved=8_000_000,
        in_specs=[SCALAR] + [WHOLE] * 4,
        scratch_shapes=[pltpu.VMEM((H, 3 * C, 128), F32)],
    )(side, *[in_hbm(x) for x in args])


def pair_grad(b, ds, inv, bias, n, wt, done):
    groups = GROUPS
    spec = lambda *tail: pl.BlockSpec((1, groups, T) + tail, lambda s: (b, s, 0, 0))
    fresh = done is None
    return call(
        lambda *refs: pair_kernel(groups, *(refs if not fresh else refs[:5] + (None,) + refs[5:])),
        [far(B, T, T, CP)],
        24,
        flops=2_000_000_000,
        moved=5_000_000,
        grid=(G // groups,),
        in_specs=[spec(128)] * 3 + [spec(WIDE), pl.BlockSpec((H, CP), lambda s: (0, 0))]
        + ([] if fresh else [pl.BlockSpec(memory_space=pltpu.HBM)]),
        out_specs=[pl.BlockSpec((1, groups * I8, T, CP), lambda s: (b, s, 0, 0))],
        scratch_shapes=[pltpu.VMEM((128, WIDE), BF16), pltpu.VMEM((128, WIDE), BF16)],
        **({} if fresh else dict(input_output_aliases={5: 0})),
    )(*[in_hbm(x) for x in (ds, inv, bias, n, wt)], *([] if fresh else [done]))[0]


def bias_out(side, got, keep, more, after):
    half = f32(C, 128)
    return call(
        bias_out_kernel,
        [bf16(DEPTH, 3 * C + H, 128), half, half],
        16,
        in_specs=[SCALAR] + [WHOLE] * 3 + [pl.BlockSpec(memory_space=pltpu.HBM)],
    )(side, got, keep, more, in_hbm(after))


def queries_out(side, own, other):
    return call(queries_out_kernel, [f32(B, C, T)], 16, in_specs=[SCALAR] + [WHOLE] * 2)(
        side, own, other
    )[0]


def keys_out(got):
    half = f32(B, C, T)
    return call(keys_out_kernel, [half, half, f32(H, CP)], 16)(got)


ROUTE = (
    "58b92a73e4d1c60f",
    "1986b504d32cf7ea",
    "db0a9542736e1f8c",
    "a8b163d74e5fc290",
    "0a71fcdbe6498253",
    "f32ecda57b861940",
    "352c1def8b6a9704",
    "745d0cfe28196a3b",
    "c695e478103f2adb",
    "d54a9762b1e0f38c",
    "f986a704c523d1eb",
    "eb7d48910263ac5f",
    "16fe0ad982bc5437",
    "73e01fc859ab462d",
    "f1253da0cb84e976",
    "c039e21bfad54876",
)


def key_route():
    return [
        (col * PEERS + k, int(digit, 16) * PEERS + col)
        for col, line in enumerate(ROUTE)
        for k, digit in enumerate(line)
    ]


def spread_over(x, axis, groups=None):
    return lax.all_to_all(x, axis, 0, 0, tiled=True, axis_index_groups=groups)


def swap_y(x):
    return lax.ppermute(x, "row", [(r, r ^ 1) for r in range(PEERS)])


def shards(query_in, key_in, value_in, pair, bias_weight, d_out):
    route = key_route()
    k = lax.ppermute(key_in, ("row", "col"), route)
    v = lax.ppermute(value_in, ("row", "col"), route)
    wt = bias_weight.T
    side = (lax.axis_index("row") & 1).astype(jnp.int32).reshape(1)
    qt, gt, pick, turn = expanded(query_in, d_out)
    side, qt = lax.optimization_barrier((side, qt))
    n, bias, low_bias, inv = norm(pair, wt)
    scaled_scores, dw, stats = logits(k, v, qt, gt, bias)
    stats = spread_over(stats, "col")
    four, w, ds, send = scores(stats, scaled_scores, dw, k, pick, turn, n)
    planes = [list(range(z * PLANE, (z + 1) * PLANE)) for z in range(DEPTH)]
    got = spread_over(send, ("row", "col"), planes)
    keep, give = grads(side, four, w, query_in, d_out)
    d_pair = pair_grad(0, ds, inv, low_bias, n, wt, None)
    send, own, other = bias_out(side, got, keep, swap_y(give), d_pair)
    lines = [list(range(y, PEERS, 2)) for y in range(2)]
    got = spread_over(send, "row", lines)
    d_query = queries_out(side, own, swap_y(other))
    d_pair = pair_grad(1, ds, inv, low_bias, n, wt, d_pair)
    d_key, d_value, dwt = keys_out(got)
    flip = lambda x: jnp.swapaxes(x, 1, 2)
    return flip(d_query), flip(d_key), flip(d_value), d_pair, dwt.T


def solution(mesh):
    rows = P(None, "row", None)
    tiles = P(None, "row", "col", None)
    in_specs = (rows, rows, rows, tiles, P(), rows)
    swapped = P(None, "col", "row")
    out_specs = (P(None, "row", "col"), swapped, swapped, tiles, P())
    return jax.shard_map(shards, mesh=mesh, in_specs=in_specs, out_specs=out_specs, check_vma=False)
```

```python
import math

import jax
import jax.numpy as jnp
from jax import lax
from jax.experimental import pallas as pl
from jax.experimental.pallas import tpu as pltpu
from jax.sharding import PartitionSpec as P

EPS = 1e-05
F32 = jnp.float32
BF16 = jnp.bfloat16

B = 2
H = 16
C = 24
HC = H * C
CP = 128
T = 96
G = 12
I8 = 8
WIDE = I8 * CP
QH = T * H
SCALE = 1.0 / math.sqrt(C)
PEERS = 16
PLANE = 2 * PEERS
DEPTH = 8
GROUPS = 6

NN = (((1,), (0,)), ((), ()))
NT = (((1,), (1,)), ((), ()))
TN = (((0,), (0,)), ((), ()))


def dot(left, right, dims=NN):
    return lax.dot_general(left, right, dims, preferred_element_type=F32)


def iota(shape, dim):
    return lax.broadcasted_iota(jnp.int32, shape, dim)


def head_mask():
    row_head = (iota((HC, 128), 0) * 171) >> 12
    return row_head == (iota((HC, 128), 1) & (H - 1))


def query_lanes(rows, first):
    return jnp.where(iota((rows, QH), 0) - first == (iota((rows, QH), 1) >> 4), 1.0, 0.0).astype(BF16)


def block_diagonal(tile, rows_per_block):
    row_block = iota((128, CP), 0) // rows_per_block
    zero = jnp.zeros_like(tile)
    return jnp.concatenate([jnp.where(row_block == i, tile, zero) for i in range(I8)], axis=1)


def expand(source, target):
    lanes = query_lanes(T, 0)
    mask = head_mask()
    for b in range(B):
        spread = dot(source[b], lanes, TN)
        for g in range(G):
            at = slice(g * 128, (g + 1) * 128)
            target[b, :, at] = jnp.where(mask, spread[:, at], 0.0).astype(BF16)


def expand_kernel(q_ref, g_ref, qt_ref, gt_ref, pick_ref, turn_ref):
    expand(q_ref, qt_ref)
    expand(g_ref, gt_ref)
    lane = iota((256, B * HC), 1)
    batch = jnp.where(lane >= HC, 1, 0)
    within = lane - batch * HC
    query = (within >> 7) * 32 + (within >> 2 & 3) * I8 + (within >> 4 & 7)
    pick_ref[...] = jnp.where(iota((256, B * HC), 0) == batch * 128 + query, 1.0, 0.0).astype(BF16)
    turn_ref[...] = jnp.where(iota((HC, HC), 0) == iota((HC, HC), 1), 1.0, 0.0).astype(BF16)


def lane_means(wide):
    means = [
        jnp.mean(wide[:, k * CP : (k + 1) * CP], axis=1, keepdims=True) for k in range(2)
    ]
    return jnp.concatenate([jnp.broadcast_to(m, (wide.shape[0], CP)) for m in means], axis=1)


def norm_kernel(
    groups, pair_ref, wt_ref, n_ref, bias_ref, low_bias_ref, inv_ref, ones_ref, diag_ref
):
    first = (pl.program_id(0) == 0) & (pl.program_id(1) == 0)

    @pl.when(first)
    def _():
        same = (iota((256, 256), 0) >> 7) == (iota((256, 256), 1) >> 7)
        ones_ref[...] = jnp.where(same, 1.0 / CP, 0.0).astype(BF16)
        wt = wt_ref[...].astype(F32)
        diag_ref[...] = block_diagonal(jnp.concatenate([wt] * I8, axis=0), H).astype(BF16)

    ones = ones_ref[...]
    rows = groups * T
    lane_query = iota((rows, 128), 1) >> 4
    compact = jnp.zeros((rows, 128), F32)
    bias = jnp.zeros((rows, 128), F32)
    for p in range(I8 // 2):
        x = jnp.concatenate(
            [
                jnp.concatenate([pair_ref[0, g * I8 + 2 * p], pair_ref[0, g * I8 + 2 * p + 1]], axis=1)
                for g in range(groups)
            ],
            axis=0,
        )
        wide = x.astype(F32)
        if p < I8 // 4:
            centred = wide - lane_means(wide)
            spread = dot((centred * centred).astype(BF16), ones)
        else:
            centred = wide - dot(x, ones)
            spread = lane_means(centred * centred)
        inverse = lax.rsqrt(spread + EPS)
        normed = (centred * inverse).astype(BF16)
        n_ref[0, :, :, p * 256 : (p + 1) * 256] = normed.reshape(groups, T, 256)
        for k in range(2):
            compact = jnp.where(
                lane_query == 2 * p + k, inverse[:, k * CP : (k + 1) * CP], compact
            )
        bias = bias + dot(normed, diag_ref[:, p * 256 : (p + 1) * 256], NT)
    inv_ref[0] = compact.reshape(groups, T, 128).astype(BF16)
    bias = bias.reshape(groups, T, 128)
    bias_ref[0] = bias
    low_bias_ref[0] = (bias * (1.0 / CP)).astype(BF16)


def logits_kernel(k_ref, v_ref, qt_ref, gt_ref, bias_ref, logits_ref, dw_ref, stats_ref):
    for b in range(B):
        scores = dot(k_ref[b], qt_ref[b])
        inner = dot(v_ref[b], gt_ref[b])
        for g in range(G):
            at = slice(g * 128, (g + 1) * 128)
            logits = scores[:, at] * SCALE + bias_ref[b, g]
            dw = inner[:, at]
            logits_ref[b, g] = logits
            dw_ref[b, g] = dw
            top = jnp.max(logits, axis=0, keepdims=True)
            expo = jnp.exp(logits - top)
            total = jnp.sum(expo, axis=0, keepdims=True)
            level = top + jnp.log(total)
            balance = jnp.sum(expo * dw, axis=0, keepdims=True) / total
            row = b * 2 * G + g
            stats_ref[:, row : row + 1, :] = jnp.broadcast_to(level[None], (PEERS, 1, 128))
            stats_ref[:, row + G : row + G + 1, :] = jnp.broadcast_to(balance[None], (PEERS, 1, 128))


def four_query(shape, dim):
    lane = iota(shape, dim)
    return (lane >> 7) * 32 + (lane >> 2 & 3) * I8 + (lane >> 4 & 7)


def four_heads(parts, q):
    slot = iota((T, 128), 1) >> 2 & 3
    tiles = []
    for wide in range(G // 4):
        tile = parts[wide * 4 + q]
        for k in range(4):
            if k != q:
                moved = pltpu.roll(parts[wide * 4 + k], (4 * (k - q)) % 128, 1)
                tile = jnp.where(slot == k, moved, tile)
        tiles.append(tile.astype(BF16))
    return jnp.concatenate(tiles, axis=1)


def scores_kernel(
    stats_ref, logits_ref, dw_ref, k_ref, pick_ref, turn_ref, n_ref,
    four_out, w_out, ds_out, send_ref,
    ds_ref, four_ref, w_ref, sems,
):
    keep = (iota((HC // 4, HC), 0) * 171) >> 12 == (iota((HC // 4, HC), 1) & 3)
    pairs = ((four_ref, four_out), (w_ref, w_out), (ds_ref, ds_out))
    stores = []
    for b in range(B):
        levels = stats_ref[:, b * 2 * G : b * 2 * G + G, :]
        balances = stats_ref[:, b * 2 * G + G : (b + 1) * 2 * G, :]
        top = jnp.max(levels, axis=0)
        parts = jnp.exp(levels - top[None])
        total = jnp.sum(parts, axis=0)
        level = top + jnp.log(total)
        balance = jnp.sum(parts * balances, axis=0) / total
        lows = []
        for g in range(G):
            weights = jnp.exp(logits_ref[b, g] - level[g : g + 1])
            low = (weights * (dw_ref[b, g] - balance[g : g + 1])).astype(BF16)
            ds_ref[b, g] = low
            w_ref[b, g] = weights.astype(BF16)
            lows.append(low.astype(F32))
        for q in range(4):
            four_ref[b, q] = four_heads(lows, q)
        for i, (x, y) in enumerate(pairs):
            store = pltpu.make_async_copy(x.at[b], y.at[b], sems.at[b * 3 + i])
            store.start()
            stores.append(store)

    chosen = []
    for b in range(B):
        k_turned = dot(turn_ref[...], k_ref[b], NT).astype(BF16)
        quarters = []
        for q in range(4):
            spread = dot(k_turned[q * HC // 4 : (q + 1) * HC // 4], four_ref[b, q])
            quarters.append(jnp.where(keep, spread, 0.0).astype(BF16))
        chosen.append(jnp.concatenate(quarters, axis=0))
    queries = dot(jnp.concatenate(chosen, axis=1), pick_ref[...], NT) * SCALE

    total = jnp.zeros((128, WIDE), F32)
    for b in range(B):
        total = total + dot(ds_ref[b].reshape(G * T, 128), n_ref[b].reshape(G * T, WIDE), TN)
    dwt = jnp.zeros((H, CP), F32)
    for i in range(I8):
        dwt = dwt + total[i * H : (i + 1) * H, i * CP : (i + 1) * CP]
    for half in range(B):
        for h in range(H):
            own = queries[h * C : (h + 1) * C, half * 128 : (half + 1) * 128]
            send_ref[half * PEERS + h] = jnp.concatenate([own, dwt], axis=0).astype(BF16)
    for store in stores:
        store.wait()


def grads_kernel(side_ref, four_ref, w_ref, q_ref, g_ref, keep_ref, give_ref, all_ref):
    lanes = jnp.where(iota((T, HC), 0) == four_query((T, HC), 1), 1.0, 0.0).astype(BF16)
    row_head = (iota((HC, HC), 0) * 171) >> 12
    mask = (row_head & 3) == (iota((HC, HC), 1) & 3)

    def select(source):
        return jnp.where(mask, dot(source, lanes, TN), 0.0).astype(BF16)

    def gather(left, fours):
        quarter = HC // 4
        return jnp.concatenate(
            [dot(left[q * quarter : (q + 1) * quarter], fours[q], NT) for q in range(4)], axis=0
        )

    keys, values = [], []
    for b in range(B):
        keys.append(gather(select(q_ref[b]), [four_ref[b, q] for q in range(4)]) * SCALE)
        parts = [w_ref[b, g].astype(F32) for g in range(G)]
        values.append(gather(select(g_ref[b]), [four_heads(parts, q) for q in range(4)]))
    kv = jnp.concatenate(keys + values, axis=1)
    for h in range(H):
        for t in range(3):
            all_ref[h, t * C : (t + 1) * C, :] = kv[h * C : (h + 1) * C, t * 128 : (t + 1) * 128]
    y_lo = side_ref[0]
    for z in range(DEPTH):
        keep_ref[z] = all_ref[2 * z + y_lo].astype(BF16)
        give_ref[z] = all_ref[2 * z + 1 - y_lo].astype(BF16)


def pair_kernel(
    groups, ds_ref, inv_ref, bias_ref, n_ref, wt_ref, _, out_ref, ones_ref, diag_ref
):
    first = pl.program_id(0) == 0

    @pl.when(first)
    def _():
        ones_ref[...] = block_diagonal(jnp.ones((128, CP), F32), H).astype(BF16)
        wt = wt_ref[...].astype(F32)
        wt = wt - jnp.mean(wt, axis=1, keepdims=True)
        diag_ref[...] = block_diagonal(jnp.concatenate([wt] * I8, axis=0), H).astype(BF16)

    rows = groups * T
    scaled = ds_ref[0].astype(F32) * inv_ref[0].astype(F32)
    along = (scaled * bias_ref[0].astype(F32)).astype(BF16).reshape(rows, 128)
    scaled = scaled.astype(BF16).reshape(rows, 128)
    for p in range(I8 // 2):
        at = slice(p * 256, (p + 1) * 256)
        back = dot(scaled, diag_ref[:, at])
        normed = n_ref[0, :, :, at].reshape(rows, 256).astype(F32)
        grad = (back - normed * dot(along, ones_ref[:, at])).astype(BF16)
        for g in range(groups):
            for k in range(2):
                out_ref[0, g * I8 + 2 * p + k] = grad[g * T : (g + 1) * T, k * CP : (k + 1) * CP]


def bias_out_kernel(side_ref, got_ref, keep_ref, more_ref, _, send_ref, own_ref, other_ref):
    dwt = jnp.sum(got_ref[:, C : C + H, :].astype(F32), axis=0)
    for z in range(DEPTH):
        kv = keep_ref[z].astype(F32) + more_ref[z].astype(F32)
        send_ref[z] = jnp.concatenate([kv, dwt], axis=0).astype(BF16)
    parts = [
        jnp.sum(got_ref[y * PEERS : (y + 1) * PEERS, 0:C, :].astype(F32), axis=0) for y in range(2)
    ]
    first = side_ref[0] == 0
    own_ref[...] = jnp.where(first, parts[0], parts[1])
    other_ref[...] = jnp.where(first, parts[1], parts[0])


def queries_out_kernel(side_ref, own_ref, other_ref, query_ref):
    first = side_ref[0] == 0
    own, other = own_ref[:, 0:T], other_ref[:, 0:T]
    query_ref[0] = jnp.where(first, own, other)
    query_ref[1] = jnp.where(first, other, own)


def keys_out_kernel(got_ref, key_ref, value_ref, dwt_ref):
    total = jnp.sum(got_ref[...].astype(F32), axis=0)
    kv = jnp.concatenate([total[t * C : (t + 1) * C] for t in range(3)], axis=1)
    for b in range(B):
        key_ref[b] = kv[:, b * T : (b + 1) * T]
        value_ref[b] = kv[:, (B + b) * T : (B + b + 1) * T]
    dwt_ref[...] = total[3 * C :]


def call(kernel, outs, limit, flops=0, moved=0, **kw):
    return pl.pallas_call(
        kernel,
        out_shape=outs,
        compiler_params=pltpu.CompilerParams(vmem_limit_bytes=limit << 20),
        cost_estimate=pl.CostEstimate(flops=flops, bytes_accessed=moved, transcendentals=0),
        **kw,
    )


def f32(*shape):
    return jax.ShapeDtypeStruct(shape, F32)


def bf16(*shape):
    return jax.ShapeDtypeStruct(shape, BF16)


def far(*shape):
    return pltpu.HBM(shape, BF16)


def in_hbm(x):
    return pltpu.with_memory_space_constraint(x, pltpu.HBM)


WHOLE = pl.BlockSpec(memory_space=pltpu.VMEM)
SCALAR = pl.BlockSpec(memory_space=pltpu.SMEM)


def expanded(query, grad):
    shape = bf16(B, HC, QH)
    outs = [shape, shape, bf16(256, B * HC), bf16(HC, HC)]
    return call(expand_kernel, outs, 16, flops=400_000_000, moved=5_000_000)(query, grad)


def norm(pair, wt):
    groups = GROUPS
    spec = lambda *tail: pl.BlockSpec((1, groups, T) + tail, lambda b, s: (b, s, 0, 0))
    return call(
        lambda *refs: norm_kernel(groups, *refs),
        [far(B, G, T, WIDE), f32(B, G, T, 128), far(B, G, T, 128), far(B, G, T, 128)],
        24,
        flops=4_000_000_000,
        moved=12_000_000,
        grid=(B, G // groups),
        in_specs=[
            pl.BlockSpec((1, groups * I8, T, CP), lambda b, s: (b, s, 0, 0)),
            pl.BlockSpec((H, CP), lambda b, s: (0, 0)),
        ],
        out_specs=[spec(WIDE), spec(128), spec(128), spec(128)],
        scratch_shapes=[pltpu.VMEM((256, 256), BF16), pltpu.VMEM((128, WIDE), BF16)],
    )(in_hbm(pair), in_hbm(wt))


def logits(k, v, qt, gt, bias):
    big = f32(B, G, T, 128)
    return call(
        logits_kernel, [big, big, f32(PEERS, 4 * G, 128)], 16, flops=1_000_000_000, moved=8_000_000
    )(k, v, qt, gt, bias)


def scores(*args):
    cell = far(B, G, T, 128)
    hbm = pl.BlockSpec(memory_space=pltpu.HBM)
    return call(
        scores_kernel,
        [far(B, 4, T, HC), cell, cell, bf16(PLANE, C + H, 128)],
        24,
        flops=2_500_000_000,
        moved=8_000_000,
        in_specs=[WHOLE] * 7,
        out_specs=[hbm] * 3 + [WHOLE],
        scratch_shapes=[
            pltpu.VMEM((B, G, T, 128), BF16),
            pltpu.VMEM((B, 4, T, HC), BF16),
            pltpu.VMEM((B, G, T, 128), BF16),
            pltpu.SemaphoreType.DMA((3 * B,)),
        ],
    )(*args)


def grads(side, *args):
    half = bf16(DEPTH, 3 * C, 128)
    return call(
        grads_kernel,
        [half, half],
        24,
        flops=2_500_000_000,
        moved=8_000_000,
        in_specs=[SCALAR] + [WHOLE] * 4,
        scratch_shapes=[pltpu.VMEM((H, 3 * C, 128), F32)],
    )(side, *[in_hbm(x) for x in args])


def pair_grad(b, ds, inv, bias, n, wt, done):
    groups = GROUPS
    spec = lambda *tail: pl.BlockSpec((1, groups, T) + tail, lambda s: (b, s, 0, 0))
    fresh = done is None
    return call(
        lambda *refs: pair_kernel(groups, *(refs if not fresh else refs[:5] + (None,) + refs[5:])),
        [far(B, T, T, CP)],
        24,
        flops=2_000_000_000,
        moved=5_000_000,
        grid=(G // groups,),
        in_specs=[spec(128)] * 3 + [spec(WIDE), pl.BlockSpec((H, CP), lambda s: (0, 0))]
        + ([] if fresh else [pl.BlockSpec(memory_space=pltpu.HBM)]),
        out_specs=[pl.BlockSpec((1, groups * I8, T, CP), lambda s: (b, s, 0, 0))],
        scratch_shapes=[pltpu.VMEM((128, WIDE), BF16), pltpu.VMEM((128, WIDE), BF16)],
        **({} if fresh else dict(input_output_aliases={5: 0})),
    )(*[in_hbm(x) for x in (ds, inv, bias, n, wt)], *([] if fresh else [done]))[0]


def bias_out(side, got, keep, more, after):
    half = f32(C, 128)
    return call(
        bias_out_kernel,
        [bf16(DEPTH, 3 * C + H, 128), half, half],
        16,
        in_specs=[SCALAR] + [WHOLE] * 3 + [pl.BlockSpec(memory_space=pltpu.HBM)],
    )(side, got, keep, more, in_hbm(after))


def queries_out(side, own, other):
    return call(queries_out_kernel, [f32(B, C, T)], 16, in_specs=[SCALAR] + [WHOLE] * 2)(
        side, own, other
    )[0]


def keys_out(got):
    half = f32(B, C, T)
    return call(keys_out_kernel, [half, half, f32(H, CP)], 16)(got)


ROUTE = (
    "58b92a73e4d1c60f",
    "1986b504d32cf7ea",
    "db0a9542736e1f8c",
    "a8b163d74e5fc290",
    "0a71fcdbe6498253",
    "f32ecda57b861940",
    "352c1def8b6a9704",
    "745d0cfe28196a3b",
    "c695e478103f2adb",
    "d54a9762b1e0f38c",
    "f986a704c523d1eb",
    "eb7d48910263ac5f",
    "16fe0ad982bc5437",
    "73e01fc859ab462d",
    "f1253da0cb84e976",
    "c039e21bfad54876",
)


def key_route():
    return [
        (col * PEERS + k, int(digit, 16) * PEERS + col)
        for col, line in enumerate(ROUTE)
        for k, digit in enumerate(line)
    ]


def spread_over(x, axis, groups=None):
    return lax.all_to_all(x, axis, 0, 0, tiled=True, axis_index_groups=groups)


def swap_y(x):
    return lax.ppermute(x, "row", [(r, r ^ 1) for r in range(PEERS)])


def shards(query_in, key_in, value_in, pair, bias_weight, d_out):
    route = key_route()
    k = lax.ppermute(key_in, ("row", "col"), route)
    v = lax.ppermute(value_in, ("row", "col"), route)
    wt = bias_weight.T
    side = (lax.axis_index("row") & 1).astype(jnp.int32).reshape(1)
    qt, gt, pick, turn = expanded(query_in, d_out)
    side, qt = lax.optimization_barrier((side, qt))
    n, bias, low_bias, inv = norm(pair, wt)
    scaled_scores, dw, stats = logits(k, v, qt, gt, bias)
    stats = spread_over(stats, "col")
    four, w, ds, send = scores(stats, scaled_scores, dw, k, pick, turn, n)
    planes = [list(range(z * PLANE, (z + 1) * PLANE)) for z in range(DEPTH)]
    got = spread_over(send, ("row", "col"), planes)
    keep, give = grads(side, four, w, query_in, d_out)
    d_pair = pair_grad(0, ds, inv, low_bias, n, wt, None)
    send, own, other = bias_out(side, got, keep, swap_y(give), d_pair)
    lines = [list(range(y, PEERS, 2)) for y in range(2)]
    got = spread_over(send, "row", lines)
    d_query = queries_out(side, own, swap_y(other))
    d_pair = pair_grad(1, ds, inv, low_bias, n, wt, d_pair)
    d_key, d_value, dwt = keys_out(got)
    flip = lambda x: jnp.swapaxes(x, 1, 2)
    return flip(d_query), flip(d_key), flip(d_value), d_pair, dwt.T


def solution(mesh):
    rows = P(None, "row", None)
    tiles = P(None, "row", "col", None)
    in_specs = (rows, rows, rows, tiles, P(), rows)
    swapped = P(None, "col", "row")
    out_specs = (P(None, "row", "col"), swapped, swapped, tiles, P())
    return jax.shard_map(shards, mesh=mesh, in_specs=in_specs, out_specs=out_specs, check_vma=False)
```
